32 devices in a mesh: rve: 4 (over z), gy: 2 (over x), gz: 4 (over y, core).
Axes of the slice: x: 2, y: 2, z: 4, core: 2. Of those that a mesh axis runs over, the one named last changes fastest.
Arguments:
- strain: float32 [32, 6], P('rve'), may hold values from -6 to 6
- tangent: float32 [32], P('rve'), may hold values from 0.5 to 2
- yield_list: int32 [16], P('rve'), may hold values from 0 to 7, as said below
- destination: int32 [16, 1], P('rve'), may hold values from 0 to 3; in each aligned block of 4 rows (0 to 3, 4 to 7, ...) at most 2 rows name the same one
- phase_map: int32 [4, 8, 32, 128], P('rve', 'gy', 'gz'), may hold values from 0 to 1
- polarization: float32 [4, 3, 6, 8, 32, 128], P('rve', None, None, 'gy', 'gz'), may hold values from -6 to 6
- stencil: float32 [3, 3, 27], replicated, may hold values from -0.6 to 3, as said below
Outputs:
- fields: float32 [4, 8, 3, 8, 32, 128], P('rve', None, None, 'gy', 'gz')
- stress_rows: float32 [16, 6], P('rve')
The draws below stay inside these ranges and needn't reach their ends.
Inputs may be any that keep to these rules, and one draw needn't show every extreme that they name: `yield_list`: the 4 entries of each macro device are distinct local point numbers, and each device lists 0 and 7. `destination`: among the 4 entries of one macro device, no group is named more than 2 times. stencil[c, d, o] equals stencil[d, c, 26 - o] for all channels and offsets.
All inputs are finite; a program needn't handle non-finite values.
Results may differ from the reference program's by a relative error of at most 0.0003.
Values sent between devices are 32-bit elements; how exact they have to be, the bound alone decides.
A program may use at most 192 MiB of HBM per device.

```python
import math
import jax
import jax.numpy as jnp
import numpy as np
from jax import lax

NX = 128
ROWS_DEV = 8
YLD = 4
CAP = 2
SWEEPS = 6
NY = 8
NZ = 32
LOADS = 8
MACRO = 32
YROWS = 16
N_RVE = 4


CENTRE_VALUE = 3.0


FACE_BASE = 0.085


FACE_ALONG = 0.1


EDGE_WEIGHT = 0.01


CORNER_WEIGHT = 0.004


CROSS_EDGE = 0.004


CROSS_CORNER = 0.002


def draw_stencil(key, part):
    offsets = jnp.arange(27, dtype=jnp.int32)
    components = jnp.stack([offsets // 9 - 1, offsets // 3 % 3 - 1, offsets % 3 - 1], axis=0).astype(jnp.float32)
    moving = jnp.abs(components[0]) + jnp.abs(components[1]) + jnp.abs(components[2])
    is_face = (moving == 1.0).astype(jnp.float32)
    is_edge = (moving == 2.0).astype(jnp.float32)
    is_corner = (moving == 3.0).astype(jnp.float32)
    same_channel = jnp.eye(3, dtype=jnp.float32)[:, :, None]
    along_channel = jnp.abs(components)
    own_part = -(FACE_BASE + FACE_ALONG * along_channel) * is_face[None, :] - EDGE_WEIGHT * is_edge[None, :] - CORNER_WEIGHT * is_corner[None, :]
    product = components[:, None, :] * components[None, :, :]
    cross_part = -(CROSS_EDGE * is_edge + CROSS_CORNER * is_corner)[None, None, :] * product * (1.0 - same_channel)
    pattern = same_channel * own_part[:, None, :] + cross_part
    raw_factors = jax.random.uniform(key, (3, 3, 27), jnp.float32, 0.85, 1.0)
    factors = 0.5 * (raw_factors + jnp.transpose(raw_factors, (1, 0, 2))[:, :, ::-1])
    centre = same_channel * (offsets == 13).astype(jnp.float32)[None, None, :]
    return CENTRE_VALUE * (pattern * factors + centre)


def draw_yield_list(key, part):
    block_count = YROWS // YLD
    block_keys = jax.random.split(key, block_count)

    def one_block(block_key):
        first_key, second_key = jax.random.split(block_key)
        middle = 1 + jax.random.permutation(first_key, ROWS_DEV - 2)[:YLD - 2]
        chosen = jnp.concatenate([jnp.array([0, ROWS_DEV - 1], dtype=jnp.int32), middle.astype(jnp.int32)])
        return chosen[jax.random.permutation(second_key, YLD)]
    return jax.vmap(one_block)(block_keys).reshape(YROWS).astype(jnp.int32)


def plant(drawn, rng, least, high):
    place = [jax.random.randint(jax.random.fold_in(rng, axis), (), 0, length) for axis, length in enumerate(drawn.shape)]
    widest = drawn.shape.index(max(drawn.shape))
    next_to = place[:widest] + [(place[widest] + 1) % drawn.shape[widest]] + place[widest + 1:]
    return drawn.at[tuple(place)].set(least).at[tuple(next_to)].set(high)


def block_levels(rng, shape, cuts, low, high):
    factor_of = 1.0
    for position, blocks in cuts:
        steps = jax.random.uniform(jax.random.fold_in(jax.random.fold_in(rng, 6), position), (blocks,), jnp.float32, low / len(cuts), high / len(cuts))
        factor_of = factor_of * jnp.repeat(jnp.exp(steps), shape[position] // blocks).reshape((-1,) + (1,) * (len(shape) - 1 - position))
    return factor_of


def assign_block(own_key, own, number, rows, number_of, top, reach, slope):
    order = jax.random.permutation(own_key, number_of)
    crowded, usual = shares(number_of, rows * top, reach, slope, True), shares(number_of, rows * top, reach, slope, False)
    places = jnp.arange(number_of)

    def named(tallies, rotation):
        used = int((tallies > 0).sum())
        fixed = max(1, used // 4)
        passed = fixed + (places - fixed + rotation * (used - fixed)) % max(1, number_of - fixed)
        return jnp.zeros((number_of,), jnp.int32).at[order[jnp.where(places < fixed, places, passed)]].set(jnp.asarray(tallies, jnp.int32))

    tallies = jnp.where(number % 4 == 0, named(crowded, number // 4), named(usual, number - number // 4 - 1))
    mixed = jax.random.permutation(jax.random.fold_in(own, 3), number_of)
    giver, receiver = mixed[0:number_of // 2 * 2:2], mixed[1:number_of // 2 * 2:2]
    margin = jnp.minimum(tallies[giver] - 1, reach - tallies[receiver]) // 2
    margin = jnp.where((giver == order[0]) | (receiver == order[0]) | (tallies[receiver] == 0), 0, jnp.maximum(margin, 0))
    passed = jax.random.randint(jax.random.fold_in(own, 4), (number_of // 2,), 0, 1 << 20) % (margin + 1)
    tallies = tallies.at[giver].add(-passed).at[receiver].add(passed)
    labels = jnp.searchsorted(jnp.cumsum(tallies), jnp.arange(rows * top), side="right").astype(jnp.int32)
    grid = labels.reshape(top, rows).T
    grid = grid[jax.random.permutation(jax.random.fold_in(own, 1), rows)]
    rotation = jax.random.randint(jax.random.fold_in(own, 2), (rows, 1), 0, top)
    return jnp.take_along_axis(grid, (jnp.arange(top)[None, :] + rotation) % top, axis=1)


def shares(count, total, reach, slope, full):
    portions = [(1 << 20) // math.isqrt(standing ** slope) + 1 for standing in range(1, count + 1)]
    largest = reach if full else min(reach, max(-(-total // count), total * portions[0] // sum(portions)))
    least = 1 if total - largest >= count - 1 else 0
    counts, spare = [largest] + [least] * (count - 1), total - largest - least * (count - 1)
    while spare > 0:
        candidates = [i for i in range(1, count) if counts[i] < largest] or [i for i in range(1, count) if counts[i] < reach]
        mass, budget = sum([portions[i] for i in candidates]), spare
        for i in candidates:
            extra = min(reach - counts[i], max(1, budget * portions[i] // mass), spare)
            counts[i] = counts[i] + extra
            spare = spare - extra
    return np.array(counts)


def noise(rng, extent, deviation, reach, cuts=(), kind=jnp.bfloat16):
    drawn = deviation * jax.random.normal(rng, extent, jnp.float32)
    if cuts:
        drawn = drawn * block_levels(rng, extent, cuts, -0.22, 0.18)
    return jnp.clip(drawn, -reach, reach).astype(kind)


def setup_inputs(seed: int = 0) -> dict:
    seeds = jax.random.split(jax.random.key(seed), 8)
    strain = noise(seeds[0], (MACRO, 6), 1.0, 6.0, ((0, 4),), jnp.float32)
    tangent = jnp.clip(jnp.exp(math.log(2.0) - 1.3862944 * jax.random.uniform(seeds[1], (MACRO,), jnp.float32) ** block_levels(seeds[1], (MACRO,), ((0, 4),), -0.2, 0.2)), 0.5, 2.0)
    yield_list = draw_yield_list(jax.random.fold_in(seeds[7], 71), 0)
    destination_keys = jax.random.split(jax.random.fold_in(seeds[3], 1), YROWS // YLD)
    destination_turns = jax.random.permutation(jax.random.fold_in(seeds[3], 3), YROWS // YLD)
    destination = jax.vmap(lambda own, number: assign_block(jax.random.fold_in(seeds[3], 2), own, number, YLD, N_RVE, 1, CAP, 2))(destination_keys, destination_turns).reshape((YROWS, 1))
    phase_map = plant(jax.random.randint(seeds[4], (N_RVE, NY, NZ, NX), 0, 2), jax.random.fold_in(seeds[4], 1), 0, 1).astype(jnp.int32)
    polarization = noise(seeds[5], (N_RVE, 3, 6, NY, NZ, NX), 1.0, 6.0, ((0, 4), (3, 2), (4, 4)), jnp.float32)
    stencil = draw_stencil(jax.random.fold_in(seeds[7], 71), 0)
    return dict(strain=strain, tangent=tangent, yield_list=yield_list, destination=destination, phase_map=phase_map, polarization=polarization, stencil=stencil)


FULL_PRECISION = lax.Precision.HIGHEST
LOWER_BOUND = 0.05
UPPER_BOUND = 1.95


def chebyshev_weights(sweep_count):
    centre_value = 0.5 * (UPPER_BOUND + LOWER_BOUND)
    half_width = 0.5 * (UPPER_BOUND - LOWER_BOUND)
    ratio_value = centre_value / half_width
    rho_before = 1.0 / ratio_value
    weights = []
    for sweep_index in range(1, sweep_count):
        rho_after = 1.0 / (2.0 * ratio_value - rho_before)
        weights.append((rho_after * rho_before, 2.0 * rho_after / half_width))
        rho_before = rho_after
    return 1.0 / centre_value, weights


def apply_stiffness(field_now, moduli, stencil):
    inner_y = field_now.shape[2] - 2
    inner_z = field_now.shape[3] - 2
    centre_mod = moduli[:, 1:1 + inner_y, 1:1 + inner_z, :]
    running = None
    for shift_y in (-1, 0, 1):
        for shift_z in (-1, 0, 1):
            shifted = field_now[:, :, 1 + shift_y:1 + shift_y + inner_y, 1 + shift_z:1 + shift_z + inner_z, :]
            shifted_mod = moduli[:, 1 + shift_y:1 + shift_y + inner_y, 1 + shift_z:1 + shift_z + inner_z, :]
            for shift_x in (-1, 0, 1):
                if shift_x != 0:
                    rolled = jnp.roll(shifted, -shift_x, axis=4)
                    rolled_mod = jnp.roll(shifted_mod, -shift_x, axis=3)
                else:
                    rolled = shifted
                    rolled_mod = shifted_mod
                offset_index = (shift_y + 1) * 9 + (shift_z + 1) * 3 + (shift_x + 1)
                edge_mod = 0.5 * (centre_mod + rolled_mod)
                contrib = jnp.einsum("cd,ldyzx->lcyzx", stencil[:, :, offset_index], edge_mod[:, None] * rolled, precision=FULL_PRECISION)
                running = contrib if running is None else running + contrib
    return running


def solve_group(phase_group, polar_group, strain_group, tangent_group, stencil):
    moduli = jnp.where(phase_group[None] == 1, tangent_group[:, None, None, None], jnp.float32(1.0))
    body_force = moduli[:, None] * jnp.einsum("cjyzx,lj->lcyzx", polar_group, strain_group, precision=FULL_PRECISION)
    centre_diag = jnp.diagonal(stencil[:, :, 13])
    inverse_diag = 1.0 / (centre_diag[None, :, None, None, None] * moduli[:, None])
    wrapped_mod = jnp.pad(moduli, ((0, 0), (1, 1), (1, 1), (0, 0)), mode="wrap")
    first_weight, weights = chebyshev_weights(SWEEPS)
    update = first_weight * (body_force * inverse_diag)
    field_now = update
    for old_weight, new_weight in weights:
        wrapped = jnp.pad(field_now, ((0, 0), (0, 0), (1, 1), (1, 1), (0, 0)), mode="wrap")
        residual_now = body_force - apply_stiffness(wrapped, wrapped_mod, stencil)
        update = old_weight * update + new_weight * (residual_now * inverse_diag)
        field_now = field_now + update
    coupled = jnp.einsum("cjyzx,lcyzx->lj", polar_group, moduli[:, None] * field_now, precision=FULL_PRECISION)
    stress = (coupled + strain_group * jnp.sum(moduli, axis=(1, 2, 3))[:, None]) / (NY * NZ * NX)
    return field_now, stress


def reference(strain, tangent, yield_list, destination, phase_map, polarization, stencil):
    rows_index = jnp.arange(YROWS, dtype=jnp.int32)
    sender = rows_index // YLD
    group_of = destination[:, 0]
    earlier = (group_of[:, None] == group_of[None, :]) & (sender[:, None] == sender[None, :]) & (rows_index[None, :] < rows_index[:, None])
    rank_in = jnp.sum(earlier.astype(jnp.int32), axis=1)
    slot_of = sender * CAP + rank_in
    group_ids = jnp.arange(N_RVE, dtype=jnp.int32)
    slot_ids = jnp.arange(LOADS, dtype=jnp.int32)
    onehot = ((group_of[None, None, :] == group_ids[:, None, None]) & (slot_of[None, None, :] == slot_ids[None, :, None])).astype(jnp.float32)
    source = sender * ROWS_DEV + yield_list
    picker = (jnp.arange(MACRO, dtype=jnp.int32)[None, :] == source[:, None]).astype(jnp.float32)
    row_strain = jnp.dot(picker, strain, precision=FULL_PRECISION)
    row_tangent = jnp.dot(picker, tangent, precision=FULL_PRECISION)
    slot_strain = jnp.einsum("gli,ij->glj", onehot, row_strain, precision=FULL_PRECISION)
    slot_tangent = jnp.einsum("gli,i->gl", onehot, row_tangent, precision=FULL_PRECISION) + 1.0 - jnp.sum(onehot, axis=2)

    def one_group(packed):
        return solve_group(packed[0], packed[1], packed[2], packed[3], stencil)

    fields, stresses = lax.map(one_group, (phase_map, polarization, slot_strain, slot_tangent))
    stress_rows = jnp.einsum("gli,glj->ij", onehot, stresses, precision=FULL_PRECISION)
    return fields, stress_rows
```

```python
import functools

import jax
import jax.numpy as jnp
from jax import lax
from jax.experimental import pallas as pl
from jax.experimental.pallas import tpu as pltpu
from jax.sharding import PartitionSpec as P

CAP = 2
CORES = 2
SWEEPS = 6
MESH = pl.DeviceIdType.MESH
TANGENT, TARGET, RANK, LISTED = 6, 7, 8, 9


FULL_PRECISION = lax.Precision.HIGHEST
LOWER_BOUND = 0.05
UPPER_BOUND = 1.95


def padded(block, sides, width):
    for axis, dim in sides:
        count = lax.axis_size(axis)
        forward = [(i, i + 1) for i in range(count - 1)]
        forward.append((count - 1, 0))
        backward = [(target, source) for source, target in forward]
        low = lax.ppermute(
            lax.slice_in_dim(block, block.shape[dim] - width, None, axis=dim), axis, forward
        )
        high = lax.ppermute(lax.slice_in_dim(block, 0, width, axis=dim), axis, backward)
        block = jnp.concatenate([low, block, high], axis=dim)
    return block


def chebyshev_weights(sweep_count):
    centre_value = 0.5 * (UPPER_BOUND + LOWER_BOUND)
    half_width = 0.5 * (UPPER_BOUND - LOWER_BOUND)
    ratio_value = centre_value / half_width
    rho_before = 1.0 / ratio_value
    weights = []
    for sweep_index in range(1, sweep_count):
        rho_after = 1.0 / (2.0 * ratio_value - rho_before)
        weights.append((rho_after * rho_before, 2.0 * rho_after / half_width))
        rho_before = rho_after
    return (1.0 / centre_value, weights)


def trim_margin(values_in, margin_have, margin_want, first_dim):
    excess = margin_have - margin_want
    values_in = lax.slice_in_dim(
        values_in, excess, values_in.shape[first_dim] - excess, axis=first_dim
    )
    return lax.slice_in_dim(
        values_in, excess, values_in.shape[first_dim + 1] - excess, axis=first_dim + 1
    )


def apply_stiffness(field_now, moduli, stencil):
    inner_y = field_now.shape[2] - 2
    inner_z = field_now.shape[3] - 2
    centre_mod = moduli[:, 1 : 1 + inner_y, 1 : 1 + inner_z, :]
    running = [None, None, None]
    for shift_y in (-1, 0, 1):
        for shift_z in (-1, 0, 1):
            shifted = field_now[
                :, :, 1 + shift_y : 1 + shift_y + inner_y, 1 + shift_z : 1 + shift_z + inner_z, :
            ]
            shifted_mod = moduli[
                :, 1 + shift_y : 1 + shift_y + inner_y, 1 + shift_z : 1 + shift_z + inner_z, :
            ]
            for shift_x in (-1, 0, 1):
                if shift_x != 0:
                    rolled = jnp.roll(shifted, -shift_x, axis=4)
                    rolled_mod = jnp.roll(shifted_mod, -shift_x, axis=3)
                else:
                    rolled = shifted
                    rolled_mod = shifted_mod
                offset_index = (shift_y + 1) * 9 + (shift_z + 1) * 3 + (shift_x + 1)
                edge_mod = 0.5 * (centre_mod + rolled_mod)
                weighted = [edge_mod * rolled[:, channel_in] for channel_in in range(3)]
                for channel_out in range(3):
                    mixed = stencil[channel_out, 0, offset_index] * weighted[0]
                    mixed = mixed + stencil[channel_out, 1, offset_index] * weighted[1]
                    mixed = mixed + stencil[channel_out, 2, offset_index] * weighted[2]
                    if running[channel_out] is None:
                        running[channel_out] = mixed
                    else:
                        running[channel_out] = running[channel_out] + mixed
    return jnp.stack(running, axis=1)


def body(strain, tangent, yield_list, destination, phase_map, polarization, stencil):
    groups = lax.axis_size("rve")
    rows_here = strain.shape[0]
    yield_count = yield_list.shape[0]
    picker = (jnp.arange(rows_here, dtype=jnp.int32)[None, :] == yield_list[:, None]).astype(
        jnp.float32
    )
    row_strain = jnp.dot(picker, strain, precision=FULL_PRECISION)
    row_tangent = jnp.dot(picker, tangent, precision=FULL_PRECISION)
    target = destination[:, 0]
    positions = jnp.arange(yield_count, dtype=jnp.int32)
    earlier = (target[:, None] == target[None, :]) & (positions[None, :] < positions[:, None])
    rank_in = jnp.sum(earlier.astype(jnp.int32), axis=1)
    group_ids = jnp.arange(groups, dtype=jnp.int32)
    slot_ids = jnp.arange(CAP, dtype=jnp.int32)
    onehot = (
        (target[None, None, :] == group_ids[:, None, None])
        & (rank_in[None, None, :] == slot_ids[None, :, None])
    ).astype(jnp.float32)
    packet = jnp.einsum("gci,ij->gcj", onehot, row_strain, precision=FULL_PRECISION)
    packet_tangent = (
        jnp.einsum("gci,i->gc", onehot, row_tangent, precision=FULL_PRECISION)
        + 1.0
        - jnp.sum(onehot, axis=2)
    )
    parcel = jnp.concatenate([packet, packet_tangent[:, :, None]], axis=2)
    arrived = lax.all_to_all(parcel, "rve", split_axis=0, concat_axis=0, tiled=True)
    slot_strain = arrived[:, :, :6].reshape(groups * CAP, 6)
    slot_tangent = arrived[:, :, 6].reshape(groups * CAP)
    phase_wide = padded(phase_map[0], (("gy", 0), ("gz", 1)), 2)
    moduli_wide = jnp.where(
        phase_wide[None] == 1, slot_tangent[:, None, None, None], jnp.float32(1.0)
    )
    moduli_core = trim_margin(moduli_wide, 2, 0, 1)
    moduli_one = trim_margin(moduli_wide, 2, 1, 1)
    polar_local = polarization[0]
    centre_diag = jnp.diagonal(stencil[:, :, 13])
    body_force = moduli_core[:, None] * jnp.einsum(
        "cjyzx,lj->lcyzx", polar_local, slot_strain, precision=FULL_PRECISION
    )
    inverse_diag = 1.0 / (centre_diag[None, :, None, None, None] * moduli_core[:, None])
    first_weight, weights = chebyshev_weights(SWEEPS)
    update = first_weight * (body_force * inverse_diag)
    field_now = update
    for old_weight, new_weight in weights:
        wrapped = padded(field_now, (("gy", 2), ("gz", 3)), 1)
        residual_now = body_force - apply_stiffness(wrapped, moduli_one, stencil)
        update = old_weight * update + new_weight * (residual_now * inverse_diag)
        field_now = field_now + update
    coupled = jnp.einsum(
        "cjyzx,lcyzx->lj", polar_local, moduli_core[:, None] * field_now, precision=FULL_PRECISION
    )
    partial_value = coupled + slot_strain * jnp.sum(moduli_core, axis=(1, 2, 3))[:, None]
    total_cells = (
        lax.axis_size("gy")
        * lax.axis_size("gz")
        * field_now.shape[2]
        * field_now.shape[3]
        * field_now.shape[4]
    )
    summed = lax.psum(partial_value, ("gy", "gz")) / total_cells
    returned = lax.all_to_all(
        summed.reshape(groups, CAP, 6), "rve", split_axis=0, concat_axis=0, tiled=True
    )
    stress_rows = jnp.einsum("gci,gcj->ij", onehot, returned, precision=FULL_PRECISION)
    return (field_now[None], stress_rows)


def kernel(
    groups, ngy, ngz,
    strain_hbm, tangent_hbm, yield_hbm, destination_hbm, stencil_hbm, phase_hbm, polar_hbm,
    fields, rows_out,
    strain, tangent, yield_list, destination, stencil, polar, load_sem,
    tables, slots, phase_all, polar_all, force_out, force, matrix, spread, field_now, update,
    mod_mid, mod_low, mod_high, mod_inv, stress, totals,
    table_send, table_recv, phase_send, phase_recv, polar_send, polar_recv,
    relay_send, relay_recv, force_send, force_recv,
    field_send, field_recv, total_send, total_recv, own_sem,
):
    f32, bf16 = jnp.float32, jnp.bfloat16
    channels, strains = polar.shape[:2]
    y_here, z_here, nx = polar.shape[2:]
    ny, nz = y_here * ngy, z_here * ngz
    loaded = [
        pltpu.make_async_copy(source, held, load_sem.at[index])
        for index, (source, held) in enumerate(
            [
                (destination_hbm, destination), (yield_hbm, yield_list), (strain_hbm, strain),
                (tangent_hbm, tangent), (polar_hbm.at[0], polar), (stencil_hbm, stencil),
            ]
        )
    ]
    for copy in loaded:
        copy.start()
    wide = channels * nz
    slot_rows = 3 * wide
    depth = 3 * slot_rows
    listed = yield_list.shape[0]
    loads = groups * CAP
    my_r, my_y, my_z = lax.axis_index("rve"), lax.axis_index("gy"), lax.axis_index("gz")
    my_load = my_y * ngz + my_z

    def turned(base, step, count):
        return lax.rem(base + step + count, count)

    mates = [(dy, dz) for dy in list(range(1, ngy)) + [0] for dz in list(range(1, ngz)) + [0]]
    others = [mate for mate in mates if mate != (0, 0)]

    def mate_id(dy, dz):
        return {"gy": turned(my_y, dy, ngy), "gz": turned(my_z, dz, ngz)}

    def block(dy, dz):
        y_at = turned(my_y, dy, ngy) * y_here
        z_at = pl.multiple_of(turned(my_z, dz, ngz) * z_here, 8)
        return pl.ds(y_at, y_here), pl.ds(z_at, z_here)

    barrier = pltpu.get_barrier_semaphore()
    for dy, dz in others:
        pl.semaphore_signal(barrier, inc=1, device_id=mate_id(dy, dz), device_id_type=MESH)
    for step in range(1, groups):
        pl.semaphore_signal(
            barrier, inc=1, device_id={"rve": turned(my_r, step, groups)}, device_id_type=MESH
        )

    for copy in loaded[:4]:
        copy.wait()
    row_ids = lax.broadcasted_iota(jnp.int32, (8, 128), 0)
    lane_ids = lax.broadcasted_iota(jnp.int32, (8, 128), 1)
    table = jnp.zeros((8, 128), f32)
    for i in range(listed):
        point, target = yield_list[i], destination[i]
        rank = jnp.int32(0)
        for k in range(i):
            rank = rank + jnp.where(destination[k] == target, 1, 0)
        values = [strain[point, j] for j in range(strains)]
        values += [tangent[point], target.astype(f32), rank.astype(f32), jnp.float32(1.0)]
        for j, value in enumerate(values):
            table = jnp.where((row_ids == i) & (lane_ids == j), value, table)
    tables[my_r] = table

    pl.semaphore_wait(barrier, len(others) + groups - 1)

    def table_copy(step, owner):
        return pltpu.make_async_remote_copy(
            src_ref=tables.at[my_r], dst_ref=tables.at[owner],
            send_sem=table_send.at[step], recv_sem=table_recv.at[step],
            device_id={"rve": turned(my_r, step, groups)}, device_id_type=MESH,
        )

    def phase_copy(index, dy, dz):
        y_at, z_at = block(dy, dz)
        to_y, to_z = others[index]
        return pltpu.make_async_remote_copy(
            src_ref=phase_hbm.at[0], dst_ref=phase_all.at[y_at, z_at],
            send_sem=phase_send.at[index], recv_sem=phase_recv.at[index],
            device_id=mate_id(to_y, to_z), device_id_type=MESH,
        )

    twins = [(dy, dz) for dy in range(ngy) for dz in range(0, ngz, CORES)][1:]
    my_core = lax.rem(my_z, CORES)

    def block_index(dy, dz):
        return turned(my_y, dy, ngy) * ngz + turned(my_z, dz, ngz)

    def polar_copy(index, dy, dz, c):
        at = block_index(dy, dz)
        return pltpu.make_async_remote_copy(
            src_ref=polar_hbm.at[0, c], dst_ref=polar_all.at[at, c],
            send_sem=polar_send.at[index, c], recv_sem=polar_recv.at[index, c],
            device_id=mate_id(*twins[index]), device_id_type=MESH,
        )

    def relay_copy(index, dy, dz, c, turn):
        at = block_index(dy, dz + turn)
        source = polar_hbm.at[0, c] if (dy, dz) == (0, 0) else polar_all.at[at, c]
        return pltpu.make_async_remote_copy(
            src_ref=source, dst_ref=polar_all.at[at, c],
            send_sem=relay_send.at[index, c], recv_sem=relay_recv.at[index, c],
            device_id=mate_id(0, 1 - 2 * my_core), device_id_type=MESH,
        )

    def send_polar(channels_now):
        for c in channels_now:
            for index in range(len(twins)):
                polar_copy(index, 0, 0, c).start()
            relay_copy(0, 0, 0, c, 0).start()

    def relay(channels_now):
        for c in channels_now:
            for index, (dy, dz) in enumerate(twins):
                polar_copy(index, -dy, -dz, c).wait_recv()
                relay_copy(index + 1, -dy, -dz, c, 0).start()

    for step in range(1, groups):
        table_copy(step, my_r).start()
    for index in range(len(others)):
        phase_copy(index, 0, 0).start()
    own_y, own_z = block(0, 0)
    own_phase = pltpu.make_async_copy(phase_hbm.at[0], phase_all.at[own_y, own_z], own_sem.at[0])
    own_phase.start()
    send_polar(range(1))

    for step in range(1, groups):
        table_copy(step, turned(my_r, -step, groups)).wait_recv()
    for source in range(groups):
        heard = tables[source]
        named = (heard[:, TARGET : TARGET + 1] == my_r.astype(f32)) & (
            heard[:, LISTED : LISTED + 1] == 1.0
        )
        for rank in range(CAP):
            chosen = named & (heard[:, RANK : RANK + 1] == float(rank))
            line = jnp.sum(jnp.where(chosen, heard, 0.0), axis=0, keepdims=True)
            missing = 1.0 - line[:, LISTED : LISTED + 1]
            line = line + jnp.where(lane_ids[:1] == TANGENT, missing, 0.0)
            at = source * CAP + rank
            slots[at : at + 1, :] = line

    loaded[4].wait()

    def slot_value(load, index):
        return jnp.broadcast_to(slots[pl.ds(load, 1), :][:, index : index + 1], (8, 128))

    def force_copy(index, dy, dz):
        y_at, z_at = block(dy, dz)
        return pltpu.make_async_remote_copy(
            src_ref=force_out.at[index], dst_ref=force.at[:, y_at, z_at],
            send_sem=force_send.at[index], recv_sem=force_recv.at[index],
            device_id=mate_id(*others[index]), device_id_type=MESH,
        )

    for index, (dy, dz) in enumerate(mates):
        load = turned(my_y, dy, ngy) * ngz + turned(my_z, dz, ngz)
        strain_of = [slot_value(load, j) for j in range(strains)]
        for c in range(channels):
            for y in range(y_here):
                value = polar[c, 0, y] * strain_of[0]
                for j in range(1, strains):
                    value = value + polar[c, j, y] * strain_of[j]
                if (dy, dz) == (0, 0):
                    force[c, my_y * y_here + y, own_z, :] = value
                else:
                    force_out[index, c, y] = value
        if (dy, dz) != (0, 0):
            force_copy(index, 0, 0).start()

    send_polar(range(1, channels))
    own_polar = [
        pltpu.make_async_copy(
            polar_hbm.at[0], polar_all.at[block_index(0, 0)], own_sem.at[1]
        )
    ]
    own_polar[0].start()
    loaded[5].wait()
    column = lax.broadcasted_iota(jnp.int32, (1, depth), 1)
    column_y = column // slot_rows
    column_kind = lax.rem(column, slot_rows) // wide
    column_d = lax.rem(column, wide) // nz
    picks = [[(column_y == dy) & (column_d == d) for d in range(channels)] for dy in range(3)]
    z_row = lax.broadcasted_iota(jnp.int32, (nz, depth), 0)
    z_column = lax.rem(lax.broadcasted_iota(jnp.int32, (nz, depth), 1), nz)
    bands = [z_column == lax.rem(z_row + dz - 1 + nz, nz) for dz in range(3)]
    is_low = jnp.broadcast_to(column_kind, (nz, depth)) == 1
    for dx in range(3):
        for c in range(channels):
            values = jnp.zeros((nz, depth), f32)
            for dz in range(3):
                line = jnp.zeros((1, depth), f32)
                for dy in range(3):
                    for d in range(channels):
                        line = jnp.where(
                            picks[dy][d], 0.5 * stencil[c, d, dy * 9 + dz * 3 + dx], line
                        )
                values = values + jnp.where(bands[dz], line, 0.0)
            high = values.astype(bf16).astype(f32)
            low = values - high
            at = (dx * channels + c) * nz
            matrix[at : at + nz, :] = jnp.where(is_low, low, high).astype(bf16)

    for index, (dy, dz) in enumerate(others):
        phase_copy(index, -dy, -dz).wait_recv()
    own_phase.wait()
    tangent_row = slots[pl.ds(my_load, 1), :][:, TANGENT : TANGENT + 1]
    my_tangent = jnp.broadcast_to(tangent_row, (nz, nx))
    inverse_tangent = 1.0 / my_tangent
    for y in range(ny):
        second = phase_all[y] == 1
        mod = jnp.where(second, my_tangent, 1.0)
        mod_mid[y] = mod
        mod_low[y] = pltpu.roll(mod, nx - 1, 1)
        mod_high[y] = pltpu.roll(mod, 1, 1)
        mod_inv[y] = jnp.where(second, inverse_tangent, 1.0)
    ones = jnp.ones((nz, nx), f32)
    inverse_centre = [1.0 / (ones * stencil[c, c, 13]) for c in range(channels)]

    def put(buffer, y, c, value):
        both = jnp.concatenate([value, value * mod_mid[y]], axis=1)
        high = both.astype(bf16)
        low = (both - high.astype(f32)).astype(bf16)
        at = pl.multiple_of((y + 1) * slot_rows + c * nz, 16)
        spread[buffer, pl.ds(at, nz), :] = high
        spread[buffer, pl.ds(at + wide, nz), :] = high
        spread[buffer, pl.ds(at + 2 * wide, nz), :] = low

    def wrap(buffer):
        spread[buffer, 0:slot_rows, :] = spread[buffer, ny * slot_rows : (ny + 1) * slot_rows, :]
        spread[buffer, (ny + 1) * slot_rows : (ny + 2) * slot_rows, :] = spread[
            buffer, slot_rows : 2 * slot_rows, :
        ]

    for index, (dy, dz) in enumerate(others):
        force_copy(index, -dy, -dz).wait_recv()
    first_weight, weights = chebyshev_weights(SWEEPS)
    for y in range(ny):
        for c in range(channels):
            value = first_weight * (force[c, y] * inverse_centre[c])
            update[c, y] = value
            field_now[c, y] = value
            put(0, y, c, value)
    wrap(0)

    relay(range(1))

    def row_product(buffer, y):
        at = y * slot_rows if isinstance(y, int) else pl.multiple_of(y * slot_rows, 16)
        return jnp.dot(
            matrix[...], spread[buffer, pl.ds(at, depth), :], preferred_element_type=f32
        )

    def finish_row(product, buffer, y, old_weight, new_weight, last):
        for c in range(channels):
            parts = []
            for dx, mod in enumerate((mod_low, mod_mid, mod_high)):
                row = (dx * channels + c) * nz
                parts.append(
                    mod[y] * product[row : row + nz, :nx] + product[row : row + nz, nx:]
                )
            stiff = parts[1] + pltpu.roll(parts[0], 1, 1) + pltpu.roll(parts[2], nx - 1, 1)
            residual = (force[c, y] - stiff * mod_inv[y]) * inverse_centre[c]
            step = old_weight * update[c, y] + new_weight * residual
            value = field_now[c, y] + step
            field_now[c, y] = value
            if not last:
                update[c, y] = step
                put(1 - buffer, y, c, value)

    def sweep_pair(pair, carry):
        for buffer in range(2):
            k = pair * 2 + buffer
            old_weight, new_weight = jnp.float32(weights[0][0]), jnp.float32(weights[0][1])
            for position in range(1, len(weights) - 1):
                old_weight = jnp.where(k == position, weights[position][0], old_weight)
                new_weight = jnp.where(k == position, weights[position][1], new_weight)
            product = row_product(buffer, 0)
            for y in range(ny):
                later = row_product(buffer, y + 1) if y + 1 < ny else None
                finish_row(product, buffer, y, old_weight, new_weight, False)
                product = later
            wrap(1 - buffer)
        return carry

    assert len(weights) % 2 == 1
    lax.fori_loop(0, (len(weights) - 1) // 2, sweep_pair, 0)

    relay(range(1, channels))

    def field_copy(dy, dz, y, load):
        to_y, to_z = turned(my_y, dy, ngy), turned(my_z, dz, ngz)
        z_at = pl.ds(pl.multiple_of(to_z * z_here, 8), z_here)
        return pltpu.make_async_remote_copy(
            src_ref=field_now.at[:, to_y * y_here + y, z_at],
            dst_ref=fields.at[0, load, :, y],
            send_sem=field_send.at[dy, dz, y], recv_sem=field_recv.at[dy, dz, y],
            device_id={"gy": to_y, "gz": to_z}, device_id_type=MESH,
        )

    def own_field(y):
        return pltpu.make_async_copy(
            field_now.at[:, my_y * y_here + y, own_z], fields.at[0, my_load, :, y],
            own_sem.at[2 + y],
        )

    final_buffer = (len(weights) - 1) % 2
    last_rows = [
        (dy, y, turned(my_y, dy, ngy) * y_here + y)
        for dy in list(range(1, ngy)) + [0]
        for y in range(y_here)
    ]
    product = row_product(final_buffer, last_rows[0][2])
    for place, (dy, y, row) in enumerate(last_rows):
        later = None
        if place + 1 < len(last_rows):
            later = row_product(final_buffer, last_rows[place + 1][2])
        finish_row(product, final_buffer, row, weights[-1][0], weights[-1][1], True)
        product = later
        for dz in list(range(1, ngz)) + [0]:
            if (dy, dz) != (0, 0):
                field_copy(dy, dz, y, my_load).start()
            else:
                own_field(y).start()

    own_polar[0].wait()
    for c in range(channels):
        relay_copy(0, 0, 0, c, 1 - 2 * my_core).wait_recv()
        for index, (dy, dz) in enumerate(twins):
            relay_copy(index + 1, -dy, -dz, c, 1 - 2 * my_core).wait_recv()
    totals_of = [jnp.zeros((z_here, nx), f32) for _ in range(strains)]
    mod_total = jnp.zeros((z_here, nx), f32)
    for y in range(ny):
        for part in range(ngz):
            z_at = slice(part * z_here, (part + 1) * z_here)
            at = (y // y_here) * ngz + part
            mod = mod_mid[y, z_at, :]
            mod_total = mod_total + mod
            for c in range(channels):
                flux = mod * field_now[c, y, z_at, :]
                for j in range(strains):
                    totals_of[j] = totals_of[j] + polar_all[at, c, j, y % y_here] * flux

    def whole_sum(values):
        return jnp.sum(jnp.sum(values, axis=0, keepdims=True), axis=1, keepdims=True)

    line = slots[pl.ds(my_load, 1), :] * whole_sum(mod_total)
    for j in range(strains):
        line = line + jnp.where(lane_ids[:1] == j, whole_sum(totals_of[j]), 0.0)
    stress[...] = line * (1.0 / (ny * nz * nx))

    my_macro, my_rank = my_load // CAP, lax.rem(my_load, CAP)

    def total_copy(dy, dz):
        return pltpu.make_async_remote_copy(
            src_ref=stress, dst_ref=totals.at[my_r * CAP + my_rank],
            send_sem=total_send.at[dy, dz], recv_sem=total_recv.at[my_r * CAP + my_rank],
            device_id={"rve": my_macro, **mate_id(dy, dz)}, device_id_type=MESH,
        )

    def total_arrival(group, rank):
        at = group * CAP + rank
        return pltpu.make_async_remote_copy(
            src_ref=stress, dst_ref=totals.at[at],
            send_sem=total_send.at[0, 0], recv_sem=total_recv.at[at],
            device_id={"rve": turned(my_r, 1, groups)}, device_id_type=MESH,
        )

    for dy, dz in others:
        total_copy(dy, dz).start()

    @pl.when(my_macro != my_r)
    def _():
        total_copy(0, 0).start()

    @pl.when(my_macro == my_r)
    def _():
        totals[my_r * CAP + my_rank] = stress[...]

    for group in range(groups):
        for rank in range(CAP):
            @pl.when((my_r != group) | (my_load != group * CAP + rank))
            def _():
                total_arrival(group, rank).wait_recv()

    mine = tables[my_r]
    answer = jnp.zeros((8, 128), f32)
    for group in range(groups):
        for rank in range(CAP):
            chosen = (mine[:, TARGET : TARGET + 1] == float(group)) & (
                mine[:, RANK : RANK + 1] == float(rank)
            )
            answer = answer + jnp.where(chosen, totals[group * CAP + rank], 0.0)
    rows_out[...] = answer[:listed, :strains]

    @pl.when(my_macro != my_r)
    def _():
        total_copy(0, 0).wait_send()

    for c in range(channels):
        relay_copy(0, 0, 0, c, 0).wait_send()
        for index, (dy, dz) in enumerate(twins):
            polar_copy(index, 0, 0, c).wait_send()
            relay_copy(index + 1, -dy, -dz, c, 0).wait_send()
    for y in range(y_here):
        own_field(y).wait()
    for step in range(1, groups):
        table_copy(step, my_r).wait_send()
    for index, (dy, dz) in enumerate(others):
        phase_copy(index, 0, 0).wait_send()
        force_copy(index, 0, 0).wait_send()
        total_copy(dy, dz).wait_send()
        load = turned(my_y, -dy, ngy) * ngz + turned(my_z, -dz, ngz)
        for y in range(y_here):
            field_copy(dy, dz, y, my_load).wait_send()
            field_copy(dy, dz, y, load).wait_recv()


def deliver(held_fields, held_rows, fields, rows_out, sem):
    copies = [
        pltpu.make_async_copy(held_fields, fields, sem.at[0]),
        pltpu.make_async_copy(held_rows, rows_out, sem.at[1]),
    ]
    for copy in copies:
        copy.start()
    for copy in copies:
        copy.wait()


def fused_body(strain, tangent, yield_list, destination, phase_map, polarization, stencil):
    groups, ngy, ngz = (lax.axis_size(name) for name in ("rve", "gy", "gz"))
    channels = polarization.shape[1]
    strains = polarization.shape[2]
    y_here, z_here, nx = polarization.shape[3:]
    ny, nz = y_here * ngy, z_here * ngz
    loads = groups * CAP
    count = ngy * ngz
    f32 = jnp.float32
    slot_rows = 3 * channels * nz
    vmem = pl.BlockSpec(memory_space=pltpu.VMEM)
    hbm = pl.BlockSpec(memory_space=pltpu.HBM)
    cell = pltpu.VMEM((ny, nz, nx), f32)
    vector = pltpu.VMEM((channels, ny, nz, nx), f32)

    def dma(*shape):
        return pltpu.SemaphoreType.DMA(shape)

    held_fields, held_rows = pl.pallas_call(
        functools.partial(kernel, groups, ngy, ngz),
        out_shape=(
            jax.ShapeDtypeStruct((1, loads, channels, y_here, z_here, nx), f32),
            jax.ShapeDtypeStruct((yield_list.shape[0], strains), f32),
        ),
        in_specs=[hbm] * 7,
        out_specs=(vmem, vmem),
        scratch_shapes=[
            pltpu.SMEM(strain.shape, f32),
            pltpu.SMEM(tangent.shape, f32),
            pltpu.SMEM(yield_list.shape, jnp.int32),
            pltpu.SMEM(yield_list.shape, jnp.int32),
            pltpu.SMEM(stencil.shape, f32),
            pltpu.VMEM(polarization.shape[1:], f32),
            dma(6),
            pltpu.VMEM((groups, 8, 128), f32),
            pltpu.VMEM((loads, 128), f32),
            pltpu.VMEM((ny, nz, nx), jnp.int32),
            pltpu.VMEM((count, *polarization.shape[1:]), f32),
            pltpu.VMEM((count, channels, y_here, z_here, nx), f32),
            vector,
            pltpu.VMEM((3 * channels * nz, 3 * slot_rows), jnp.bfloat16),
            pltpu.VMEM((2, (ny + 2) * slot_rows, 2 * nx), jnp.bfloat16),
            vector,
            vector,
            cell, cell, cell, cell,
            pltpu.VMEM((1, 128), f32),
            pltpu.VMEM((loads, 1, 128), f32),
            dma(groups), dma(groups), dma(count), dma(count),
            dma(count // CORES, channels), dma(count // CORES, channels),
            dma(count // CORES, channels), dma(count // CORES, channels),
            dma(count), dma(count),
            dma(ngy, ngz, y_here), dma(ngy, ngz, y_here),
            dma(ngy, ngz), dma(loads), dma(2 + y_here),
        ],
        compiler_params=pltpu.CompilerParams(
            collective_id=0, has_side_effects=True, vmem_limit_bytes=40 * 1024 * 1024
        ),
    )(*[
        pltpu.with_memory_space_constraint(argument, pltpu.HBM)
        for argument in (
            strain, tangent, yield_list, destination[:, 0], stencil, phase_map, polarization
        )
    ])
    return pl.pallas_call(
        deliver,
        out_shape=(
            jax.ShapeDtypeStruct(held_fields.shape, f32),
            jax.ShapeDtypeStruct(held_rows.shape, f32),
        ),
        in_specs=[vmem, vmem],
        out_specs=(hbm, hbm),
        scratch_shapes=[dma(2)],
        compiler_params=pltpu.CompilerParams(vmem_limit_bytes=4 * 1024 * 1024),
    )(held_fields, held_rows)


def body_for(mesh):
    def chosen(*arguments):
        strain, _, yield_list, _, phase_map, _, _ = arguments
        loads = lax.axis_size("rve") * CAP
        one_load_each = lax.axis_size("gy") * lax.axis_size("gz") == loads
        tiled = phase_map.shape[2] == 8 and phase_map.shape[3] == 128 and loads == 8
        if one_load_each and tiled and yield_list.shape[0] <= 8:
            return fused_body(*arguments)
        return body(*arguments)

    return chosen


def solution(mesh):
    return jax.shard_map(
        body_for(mesh),
        mesh=mesh,
        in_specs=(
            P("rve", None),
            P("rve"),
            P("rve"),
            P("rve", None),
            P("rve", "gy", "gz", None),
            P("rve", None, None, "gy", "gz", None),
            P(),
        ),
        out_specs=(P("rve", None, None, "gy", "gz", None), P("rve", None)),
        check_vma=False,
    )
```

```python
import functools

import jax
import jax.numpy as jnp
from jax import lax
from jax.experimental import pallas as pl
from jax.experimental.pallas import tpu as pltpu
from jax.sharding import PartitionSpec as P

CAP = 2
CORES = 2
SWEEPS = 6
MESH = pl.DeviceIdType.MESH
TANGENT, TARGET, RANK, LISTED = 6, 7, 8, 9


FULL_PRECISION = lax.Precision.HIGHEST
LOWER_BOUND = 0.05
UPPER_BOUND = 1.95


def padded(block, sides, width):
    for axis, dim in sides:
        count = lax.axis_size(axis)
        forward = [(i, i + 1) for i in range(count - 1)]
        forward.append((count - 1, 0))
        backward = [(target, source) for source, target in forward]
        low = lax.ppermute(
            lax.slice_in_dim(block, block.shape[dim] - width, None, axis=dim), axis, forward
        )
        high = lax.ppermute(lax.slice_in_dim(block, 0, width, axis=dim), axis, backward)
        block = jnp.concatenate([low, block, high], axis=dim)
    return block


def chebyshev_weights(sweep_count):
    centre_value = 0.5 * (UPPER_BOUND + LOWER_BOUND)
    half_width = 0.5 * (UPPER_BOUND - LOWER_BOUND)
    ratio_value = centre_value / half_width
    rho_before = 1.0 / ratio_value
    weights = []
    for sweep_index in range(1, sweep_count):
        rho_after = 1.0 / (2.0 * ratio_value - rho_before)
        weights.append((rho_after * rho_before, 2.0 * rho_after / half_width))
        rho_before = rho_after
    return (1.0 / centre_value, weights)


def trim_margin(values_in, margin_have, margin_want, first_dim):
    excess = margin_have - margin_want
    values_in = lax.slice_in_dim(
        values_in, excess, values_in.shape[first_dim] - excess, axis=first_dim
    )
    return lax.slice_in_dim(
        values_in, excess, values_in.shape[first_dim + 1] - excess, axis=first_dim + 1
    )


def apply_stiffness(field_now, moduli, stencil):
    inner_y = field_now.shape[2] - 2
    inner_z = field_now.shape[3] - 2
    centre_mod = moduli[:, 1 : 1 + inner_y, 1 : 1 + inner_z, :]
    running = [None, None, None]
    for shift_y in (-1, 0, 1):
        for shift_z in (-1, 0, 1):
            shifted = field_now[
                :, :, 1 + shift_y : 1 + shift_y + inner_y, 1 + shift_z : 1 + shift_z + inner_z, :
            ]
            shifted_mod = moduli[
                :, 1 + shift_y : 1 + shift_y + inner_y, 1 + shift_z : 1 + shift_z + inner_z, :
            ]
            for shift_x in (-1, 0, 1):
                if shift_x != 0:
                    rolled = jnp.roll(shifted, -shift_x, axis=4)
                    rolled_mod = jnp.roll(shifted_mod, -shift_x, axis=3)
                else:
                    rolled = shifted
                    rolled_mod = shifted_mod
                offset_index = (shift_y + 1) * 9 + (shift_z + 1) * 3 + (shift_x + 1)
                edge_mod = 0.5 * (centre_mod + rolled_mod)
                weighted = [edge_mod * rolled[:, channel_in] for channel_in in range(3)]
                for channel_out in range(3):
                    mixed = stencil[channel_out, 0, offset_index] * weighted[0]
                    mixed = mixed + stencil[channel_out, 1, offset_index] * weighted[1]
                    mixed = mixed + stencil[channel_out, 2, offset_index] * weighted[2]
                    if running[channel_out] is None:
                        running[channel_out] = mixed
                    else:
                        running[channel_out] = running[channel_out] + mixed
    return jnp.stack(running, axis=1)


def body(strain, tangent, yield_list, destination, phase_map, polarization, stencil):
    groups = lax.axis_size("rve")
    rows_here = strain.shape[0]
    yield_count = yield_list.shape[0]
    picker = (jnp.arange(rows_here, dtype=jnp.int32)[None, :] == yield_list[:, None]).astype(
        jnp.float32
    )
    row_strain = jnp.dot(picker, strain, precision=FULL_PRECISION)
    row_tangent = jnp.dot(picker, tangent, precision=FULL_PRECISION)
    target = destination[:, 0]
    positions = jnp.arange(yield_count, dtype=jnp.int32)
    earlier = (target[:, None] == target[None, :]) & (positions[None, :] < positions[:, None])
    rank_in = jnp.sum(earlier.astype(jnp.int32), axis=1)
    group_ids = jnp.arange(groups, dtype=jnp.int32)
    slot_ids = jnp.arange(CAP, dtype=jnp.int32)
    onehot = (
        (target[None, None, :] == group_ids[:, None, None])
        & (rank_in[None, None, :] == slot_ids[None, :, None])
    ).astype(jnp.float32)
    packet = jnp.einsum("gci,ij->gcj", onehot, row_strain, precision=FULL_PRECISION)
    packet_tangent = (
        jnp.einsum("gci,i->gc", onehot, row_tangent, precision=FULL_PRECISION)
        + 1.0
        - jnp.sum(onehot, axis=2)
    )
    parcel = jnp.concatenate([packet, packet_tangent[:, :, None]], axis=2)
    arrived = lax.all_to_all(parcel, "rve", split_axis=0, concat_axis=0, tiled=True)
    slot_strain = arrived[:, :, :6].reshape(groups * CAP, 6)
    slot_tangent = arrived[:, :, 6].reshape(groups * CAP)
    phase_wide = padded(phase_map[0], (("gy", 0), ("gz", 1)), 2)
    moduli_wide = jnp.where(
        phase_wide[None] == 1, slot_tangent[:, None, None, None], jnp.float32(1.0)
    )
    moduli_core = trim_margin(moduli_wide, 2, 0, 1)
    moduli_one = trim_margin(moduli_wide, 2, 1, 1)
    polar_local = polarization[0]
    centre_diag = jnp.diagonal(stencil[:, :, 13])
    body_force = moduli_core[:, None] * jnp.einsum(
        "cjyzx,lj->lcyzx", polar_local, slot_strain, precision=FULL_PRECISION
    )
    inverse_diag = 1.0 / (centre_diag[None, :, None, None, None] * moduli_core[:, None])
    first_weight, weights = chebyshev_weights(SWEEPS)
    update = first_weight * (body_force * inverse_diag)
    field_now = update
    for old_weight, new_weight in weights:
        wrapped = padded(field_now, (("gy", 2), ("gz", 3)), 1)
        residual_now = body_force - apply_stiffness(wrapped, moduli_one, stencil)
        update = old_weight * update + new_weight * (residual_now * inverse_diag)
        field_now = field_now + update
    coupled = jnp.einsum(
        "cjyzx,lcyzx->lj", polar_local, moduli_core[:, None] * field_now, precision=FULL_PRECISION
    )
    partial_value = coupled + slot_strain * jnp.sum(moduli_core, axis=(1, 2, 3))[:, None]
    total_cells = (
        lax.axis_size("gy")
        * lax.axis_size("gz")
        * field_now.shape[2]
        * field_now.shape[3]
        * field_now.shape[4]
    )
    summed = lax.psum(partial_value, ("gy", "gz")) / total_cells
    returned = lax.all_to_all(
        summed.reshape(groups, CAP, 6), "rve", split_axis=0, concat_axis=0, tiled=True
    )
    stress_rows = jnp.einsum("gci,gcj->ij", onehot, returned, precision=FULL_PRECISION)
    return (field_now[None], stress_rows)


def kernel(
    groups, ngy, ngz,
    strain_hbm, tangent_hbm, yield_hbm, destination_hbm, stencil_hbm, phase_hbm, polar_hbm,
    fields, rows_out,
    strain, tangent, yield_list, destination, stencil, polar, load_sem,
    tables, slots, phase_all, polar_far, twin_field, force_out, force, matrix, spread, field_now, update,
    mod_mid, mod_low, mod_high, mod_inv, stress, totals,
    table_send, table_recv, phase_send, phase_recv, polar_send, polar_recv,
    twin_send, twin_recv, force_send, force_recv,
    field_send, field_recv, total_send, total_recv, own_sem,
):
    f32, bf16 = jnp.float32, jnp.bfloat16
    channels, strains = polar.shape[:2]
    y_here, z_here, nx = polar.shape[2:]
    ny, nz = y_here * ngy, z_here * ngz
    loaded = [
        pltpu.make_async_copy(source, held, load_sem.at[index])
        for index, (source, held) in enumerate(
            [
                (destination_hbm, destination), (yield_hbm, yield_list), (strain_hbm, strain),
                (tangent_hbm, tangent), (polar_hbm.at[0], polar), (stencil_hbm, stencil),
            ]
        )
    ]
    for copy in loaded:
        copy.start()
    wide = channels * nz
    slot_rows = 3 * wide
    depth = 3 * slot_rows
    listed = yield_list.shape[0]
    loads = groups * CAP
    my_r, my_y, my_z = lax.axis_index("rve"), lax.axis_index("gy"), lax.axis_index("gz")
    my_load = my_y * ngz + my_z

    def turned(base, step, count):
        return lax.rem(base + step + count, count)

    mates = [(dy, dz) for dy in list(range(1, ngy)) + [0] for dz in list(range(1, ngz)) + [0]]
    others = [mate for mate in mates if mate != (0, 0)]

    def mate_id(dy, dz):
        return {"gy": turned(my_y, dy, ngy), "gz": turned(my_z, dz, ngz)}

    def block(dy, dz):
        y_at = turned(my_y, dy, ngy) * y_here
        z_at = pl.multiple_of(turned(my_z, dz, ngz) * z_here, 8)
        return pl.ds(y_at, y_here), pl.ds(z_at, z_here)

    barrier = pltpu.get_barrier_semaphore()
    for dy, dz in others:
        pl.semaphore_signal(barrier, inc=1, device_id=mate_id(dy, dz), device_id_type=MESH)
    for step in range(1, groups):
        pl.semaphore_signal(
            barrier, inc=1, device_id={"rve": turned(my_r, step, groups)}, device_id_type=MESH
        )

    for copy in loaded[:4]:
        copy.wait()
    row_ids = lax.broadcasted_iota(jnp.int32, (8, 128), 0)
    lane_ids = lax.broadcasted_iota(jnp.int32, (8, 128), 1)
    table = jnp.zeros((8, 128), f32)
    for i in range(listed):
        point, target = yield_list[i], destination[i]
        rank = jnp.int32(0)
        for k in range(i):
            rank = rank + jnp.where(destination[k] == target, 1, 0)
        values = [strain[point, j] for j in range(strains)]
        values += [tangent[point], target.astype(f32), rank.astype(f32), jnp.float32(1.0)]
        for j, value in enumerate(values):
            table = jnp.where((row_ids == i) & (lane_ids == j), value, table)
    tables[my_r] = table

    pl.semaphore_wait(barrier, len(others) + groups - 1)

    def table_copy(step, owner):
        return pltpu.make_async_remote_copy(
            src_ref=tables.at[my_r], dst_ref=tables.at[owner],
            send_sem=table_send.at[step], recv_sem=table_recv.at[step],
            device_id={"rve": turned(my_r, step, groups)}, device_id_type=MESH,
        )

    def phase_copy(index, dy, dz):
        y_at, z_at = block(dy, dz)
        to_y, to_z = others[index]
        return pltpu.make_async_remote_copy(
            src_ref=phase_hbm.at[0], dst_ref=phase_all.at[y_at, z_at],
            send_sem=phase_send.at[index], recv_sem=phase_recv.at[index],
            device_id=mate_id(to_y, to_z), device_id_type=MESH,
        )

    across, along, corner = (1, 0), (0, CORES), (1, CORES)
    twins = [across, along, corner]
    my_core = lax.rem(my_z, CORES)
    turn = 1 - 2 * my_core

    def polar_copy(index, c):
        return pltpu.make_async_remote_copy(
            src_ref=polar_hbm.at[0, c], dst_ref=polar_far.at[index, c],
            send_sem=polar_send.at[index, c], recv_sem=polar_recv.at[index, c],
            device_id=mate_id(*twins[index]), device_id_type=MESH,
        )

    def onward_copy(c):
        return pltpu.make_async_remote_copy(
            src_ref=polar_far.at[my_core, c], dst_ref=polar_far.at[2, c],
            send_sem=polar_send.at[2, c], recv_sem=polar_recv.at[2, c],
            device_id=mate_id(my_core, CORES * (1 - my_core)), device_id_type=MESH,
        )

    def send_polar(channels_now):
        for c in channels_now:
            for index in range(2):
                polar_copy(index, c).start()

    def pass_on(c):
        for index in range(2):
            polar_copy(index, c).wait_recv()
        onward_copy(c).start()

    for step in range(1, groups):
        table_copy(step, my_r).start()
    for index in range(len(others)):
        phase_copy(index, 0, 0).start()
    own_y, own_z = block(0, 0)
    own_phase = pltpu.make_async_copy(phase_hbm.at[0], phase_all.at[own_y, own_z], own_sem.at[0])
    own_phase.start()
    send_polar(range(1))

    for step in range(1, groups):
        table_copy(step, turned(my_r, -step, groups)).wait_recv()
    for source in range(groups):
        heard = tables[source]
        named = (heard[:, TARGET : TARGET + 1] == my_r.astype(f32)) & (
            heard[:, LISTED : LISTED + 1] == 1.0
        )
        for rank in range(CAP):
            chosen = named & (heard[:, RANK : RANK + 1] == float(rank))
            line = jnp.sum(jnp.where(chosen, heard, 0.0), axis=0, keepdims=True)
            missing = 1.0 - line[:, LISTED : LISTED + 1]
            line = line + jnp.where(lane_ids[:1] == TANGENT, missing, 0.0)
            at = source * CAP + rank
            slots[at : at + 1, :] = line

    loaded[4].wait()

    def slot_value(load, index):
        return jnp.broadcast_to(slots[pl.ds(load, 1), :][:, index : index + 1], (8, 128))

    def force_copy(index, dy, dz):
        y_at, z_at = block(dy, dz)
        return pltpu.make_async_remote_copy(
            src_ref=force_out.at[index], dst_ref=force.at[:, y_at, z_at],
            send_sem=force_send.at[index], recv_sem=force_recv.at[index],
            device_id=mate_id(*others[index]), device_id_type=MESH,
        )

    for index, (dy, dz) in enumerate(mates):
        load = turned(my_y, dy, ngy) * ngz + turned(my_z, dz, ngz)
        strain_of = [slot_value(load, j) for j in range(strains)]
        for c in range(channels):
            for y in range(y_here):
                value = polar[c, 0, y] * strain_of[0]
                for j in range(1, strains):
                    value = value + polar[c, j, y] * strain_of[j]
                if (dy, dz) == (0, 0):
                    force[c, my_y * y_here + y, own_z, :] = value
                else:
                    force_out[index, c, y] = value
        if (dy, dz) != (0, 0):
            force_copy(index, 0, 0).start()

    send_polar(range(1, channels))
    loaded[5].wait()
    column = lax.broadcasted_iota(jnp.int32, (1, depth), 1)
    column_y = column // slot_rows
    column_kind = lax.rem(column, slot_rows) // wide
    column_d = lax.rem(column, wide) // nz
    picks = [[(column_y == dy) & (column_d == d) for d in range(channels)] for dy in range(3)]
    z_row = lax.broadcasted_iota(jnp.int32, (nz, depth), 0)
    z_column = lax.rem(lax.broadcasted_iota(jnp.int32, (nz, depth), 1), nz)
    bands = [z_column == lax.rem(z_row + dz - 1 + nz, nz) for dz in range(3)]
    is_low = jnp.broadcast_to(column_kind, (nz, depth)) == 1
    for dx in range(3):
        for c in range(channels):
            values = jnp.zeros((nz, depth), f32)
            for dz in range(3):
                line = jnp.zeros((1, depth), f32)
                for dy in range(3):
                    for d in range(channels):
                        line = jnp.where(
                            picks[dy][d], 0.5 * stencil[c, d, dy * 9 + dz * 3 + dx], line
                        )
                values = values + jnp.where(bands[dz], line, 0.0)
            high = values.astype(bf16).astype(f32)
            low = values - high
            at = (dx * channels + c) * nz
            matrix[at : at + nz, :] = jnp.where(is_low, low, high).astype(bf16)

    for index, (dy, dz) in enumerate(others):
        phase_copy(index, -dy, -dz).wait_recv()
    own_phase.wait()
    tangent_row = slots[pl.ds(my_load, 1), :][:, TANGENT : TANGENT + 1]
    my_tangent = jnp.broadcast_to(tangent_row, (nz, nx))
    inverse_tangent = 1.0 / my_tangent
    for y in range(ny):
        second = phase_all[y] == 1
        mod = jnp.where(second, my_tangent, 1.0)
        mod_mid[y] = mod
        mod_low[y] = pltpu.roll(mod, nx - 1, 1)
        mod_high[y] = pltpu.roll(mod, 1, 1)
        mod_inv[y] = jnp.where(second, inverse_tangent, 1.0)
    ones = jnp.ones((nz, nx), f32)
    inverse_centre = [1.0 / (ones * stencil[c, c, 13]) for c in range(channels)]

    def put(buffer, y, c, value):
        both = jnp.concatenate([value, value * mod_mid[y]], axis=1)
        high = both.astype(bf16)
        low = (both - high.astype(f32)).astype(bf16)
        at = pl.multiple_of((y + 1) * slot_rows + c * nz, 16)
        spread[buffer, pl.ds(at, nz), :] = high
        spread[buffer, pl.ds(at + wide, nz), :] = high
        spread[buffer, pl.ds(at + 2 * wide, nz), :] = low

    def wrap(buffer):
        spread[buffer, 0:slot_rows, :] = spread[buffer, ny * slot_rows : (ny + 1) * slot_rows, :]
        spread[buffer, (ny + 1) * slot_rows : (ny + 2) * slot_rows, :] = spread[
            buffer, slot_rows : 2 * slot_rows, :
        ]

    for index, (dy, dz) in enumerate(others):
        force_copy(index, -dy, -dz).wait_recv()
    first_weight, weights = chebyshev_weights(SWEEPS)
    for y in range(ny):
        for c in range(channels):
            value = first_weight * (force[c, y] * inverse_centre[c])
            update[c, y] = value
            field_now[c, y] = value
            put(0, y, c, value)
    wrap(0)

    pass_on(0)

    def row_product(buffer, y):
        at = y * slot_rows if isinstance(y, int) else pl.multiple_of(y * slot_rows, 16)
        return jnp.dot(
            matrix[...], spread[buffer, pl.ds(at, depth), :], preferred_element_type=f32
        )

    def finish_row(product, buffer, y, old_weight, new_weight, last):
        for c in range(channels):
            parts = []
            for dx, mod in enumerate((mod_low, mod_mid, mod_high)):
                row = (dx * channels + c) * nz
                parts.append(
                    mod[y] * product[row : row + nz, :nx] + product[row : row + nz, nx:]
                )
            stiff = parts[1] + pltpu.roll(parts[0], 1, 1) + pltpu.roll(parts[2], nx - 1, 1)
            residual = (force[c, y] - stiff * mod_inv[y]) * inverse_centre[c]
            step = old_weight * update[c, y] + new_weight * residual
            value = field_now[c, y] + step
            field_now[c, y] = value
            if not last:
                update[c, y] = step
                put(1 - buffer, y, c, value)

    def sweep_pair(pair, carry):
        for buffer in range(2):
            k = pair * 2 + buffer
            old_weight, new_weight = jnp.float32(weights[0][0]), jnp.float32(weights[0][1])
            for position in range(1, len(weights) - 1):
                old_weight = jnp.where(k == position, weights[position][0], old_weight)
                new_weight = jnp.where(k == position, weights[position][1], new_weight)
            product = row_product(buffer, 0)
            for y in range(ny):
                later = row_product(buffer, y + 1) if y + 1 < ny else None
                finish_row(product, buffer, y, old_weight, new_weight, False)
                product = later
            wrap(1 - buffer)
            for c in range(channels):
                for turn_now, passing in ((c if c else -1, pass_on),):
                    if turn_now >= 0 and turn_now % 2 == buffer:
                        pl.when(pair == turn_now // 2)(functools.partial(passing, c))
        return carry

    assert len(weights) % 2 == 1
    lax.fori_loop(0, (len(weights) - 1) // 2, sweep_pair, 0)

    sides = [(dy, dz, dz) for dy in range(1, ngy) for dz in range(ngz)]
    sides += [(0, 1, CORES), (0, 2, CORES + turn)]

    def field_copy(dy, place, dz, y, load):
        to_y, to_z = turned(my_y, dy, ngy), turned(my_z, dz, ngz)
        z_at = pl.ds(pl.multiple_of(to_z * z_here, 8), z_here)
        return pltpu.make_async_remote_copy(
            src_ref=field_now.at[:, to_y * y_here + y, z_at],
            dst_ref=fields.at[0, load, :, y],
            send_sem=field_send.at[dy, place, y], recv_sem=field_recv.at[dy, place, y],
            device_id={"gy": to_y, "gz": to_z}, device_id_type=MESH,
        )

    def twin_copy(half, row):
        z_at = pl.multiple_of((CORES * half + 1 - my_core) * z_here, 8)
        return pltpu.make_async_remote_copy(
            src_ref=field_now.at[:, row, pl.ds(z_at, z_here)],
            dst_ref=twin_field.at[half, :, row],
            send_sem=twin_send.at[half, row], recv_sem=twin_recv.at[half, row],
            device_id=mate_id(0, turn), device_id_type=MESH,
        )

    def own_field(y):
        return pltpu.make_async_copy(
            field_now.at[:, my_y * y_here + y, own_z], fields.at[0, my_load, :, y],
            own_sem.at[2 + y],
        )

    final_buffer = (len(weights) - 1) % 2
    last_rows = [
        (dy, y, turned(my_y, dy, ngy) * y_here + y)
        for dy in list(range(1, ngy)) + [0]
        for y in range(y_here)
    ]
    product = row_product(final_buffer, last_rows[0][2])
    for place, (dy, y, row) in enumerate(last_rows):
        later = None
        if place + 1 < len(last_rows):
            later = row_product(final_buffer, last_rows[place + 1][2])
        finish_row(product, final_buffer, row, weights[-1][0], weights[-1][1], True)
        product = later
        for half in range(ngz // CORES):
            twin_copy(half, row).start()
        for side, where, dz in sides:
            if side == dy:
                field_copy(dy, where, dz, y, my_load).start()
        if dy == 0:
            own_field(y).start()

    for row in range(ny):
        for half in range(ngz // CORES):
            twin_copy(half, row).wait_recv()
    for c in range(1, channels + 1):
        if c < channels:
            polar_copy(2, c).wait_recv()
        else:
            polar_copy(2, 0).wait_recv()
    twin_load = my_load + turn
    slopes = [slot_value(my_load, TANGENT), slot_value(twin_load, TANGENT)]
    totals_of = [[jnp.zeros((z_here, nx), f32) for _ in range(strains)] for _ in range(2)]
    counted = jnp.zeros((z_here, nx), f32)
    for index, (dy, dz) in enumerate([(0, 0)] + twins):
        part = lax.rem(my_z // CORES + dz // CORES, ngz // CORES)
        for y in range(y_here):
            row = turned(my_y, dy, ngy) * y_here + y
            z_at = pl.ds(pl.multiple_of((CORES * part + my_core) * z_here, 8), z_here)
            second = phase_all[row, z_at, :] == 1
            counted = counted + jnp.where(second, 1.0, 0.0)
            mods = [jnp.where(second, slope, 1.0) for slope in slopes]
            for c in range(channels):
                theirs = twin_field[part, c, row]
                if index == 0:
                    fields[0, twin_load, c, y] = theirs
                fluxes = [mods[0] * field_now[c, row, z_at, :], mods[1] * theirs]
                for j in range(strains):
                    weight = polar[c, j, y] if index == 0 else polar_far[index - 1, c, j, y]
                    for which in range(2):
                        totals_of[which][j] = totals_of[which][j] + weight * fluxes[which]

    def whole_sum(values):
        return jnp.sum(jnp.sum(values, axis=0, keepdims=True), axis=1, keepdims=True)

    second_count = whole_sum(counted)
    for which, load in enumerate((my_load, twin_load)):
        line = slots[pl.ds(load, 1), :]
        mod_sum = second_count * line[:, TANGENT : TANGENT + 1] + (
            float(len(twins) + 1) * y_here * z_here * nx - second_count
        )
        line = line * mod_sum
        for j in range(strains):
            line = line + jnp.where(lane_ids[:1] == j, whole_sum(totals_of[which][j]), 0.0)
        stress[lax.rem(load, CAP)] = line * (1.0 / (ny * nz * nx))

    my_macro = my_load // CAP

    def total_copy(dy, dz):
        return pltpu.make_async_remote_copy(
            src_ref=stress, dst_ref=totals.at[my_r, my_core],
            send_sem=total_send.at[dy, dz], recv_sem=total_recv.at[my_r, my_core],
            device_id={"rve": my_macro, **mate_id(dy, dz)}, device_id_type=MESH,
        )

    def total_arrival(group, core):
        return pltpu.make_async_remote_copy(
            src_ref=stress, dst_ref=totals.at[group, core],
            send_sem=total_send.at[0, 0], recv_sem=total_recv.at[group, core],
            device_id={"rve": turned(my_r, 1, groups)}, device_id_type=MESH,
        )

    for dy, dz in others:
        total_copy(dy, dz).start()

    @pl.when(my_macro != my_r)
    def _():
        total_copy(0, 0).start()

    @pl.when(my_macro == my_r)
    def _():
        totals[my_r, my_core] = stress[...]

    for group in range(groups):
        for core in range(CORES):
            @pl.when((my_r != group) | (my_macro != group) | (my_core != core))
            def _():
                total_arrival(group, core).wait_recv()

    mine = tables[my_r]
    answer = jnp.zeros((8, 128), f32)
    for group in range(groups):
        for rank in range(CAP):
            chosen = (mine[:, TARGET : TARGET + 1] == float(group)) & (
                mine[:, RANK : RANK + 1] == float(rank)
            )
            line = totals[group, 0, rank]
            for core in range(1, CORES):
                line = line + totals[group, core, rank]
            answer = answer + jnp.where(chosen, line, 0.0)
    rows_out[...] = answer[:listed, :strains]

    @pl.when(my_macro != my_r)
    def _():
        total_copy(0, 0).wait_send()

    for c in range(channels):
        for index in range(2):
            polar_copy(index, c).wait_send()
        onward_copy(c).wait_send()
    for y in range(y_here):
        own_field(y).wait()
    for step in range(1, groups):
        table_copy(step, my_r).wait_send()
    for index, (dy, dz) in enumerate(others):
        phase_copy(index, 0, 0).wait_send()
        force_copy(index, 0, 0).wait_send()
        total_copy(dy, dz).wait_send()
    for dy, where, dz in sides:
        load = turned(my_y, -dy, ngy) * ngz + turned(my_z, -dz, ngz)
        for y in range(y_here):
            field_copy(dy, where, dz, y, my_load).wait_send()
            field_copy(dy, where, dz, y, load).wait_recv()
    for row in range(ny):
        for half in range(ngz // CORES):
            twin_copy(half, row).wait_send()


def deliver(held_fields, held_rows, fields, rows_out, sem):
    copies = [
        pltpu.make_async_copy(held_fields, fields, sem.at[0]),
        pltpu.make_async_copy(held_rows, rows_out, sem.at[1]),
    ]
    for copy in copies:
        copy.start()
    for copy in copies:
        copy.wait()


def fused_body(strain, tangent, yield_list, destination, phase_map, polarization, stencil):
    groups, ngy, ngz = (lax.axis_size(name) for name in ("rve", "gy", "gz"))
    channels = polarization.shape[1]
    strains = polarization.shape[2]
    y_here, z_here, nx = polarization.shape[3:]
    ny, nz = y_here * ngy, z_here * ngz
    loads = groups * CAP
    count = ngy * ngz
    f32 = jnp.float32
    slot_rows = 3 * channels * nz
    vmem = pl.BlockSpec(memory_space=pltpu.VMEM)
    hbm = pl.BlockSpec(memory_space=pltpu.HBM)
    cell = pltpu.VMEM((ny, nz, nx), f32)
    vector = pltpu.VMEM((channels, ny, nz, nx), f32)

    def dma(*shape):
        return pltpu.SemaphoreType.DMA(shape)

    held_fields, held_rows = pl.pallas_call(
        functools.partial(kernel, groups, ngy, ngz),
        out_shape=(
            jax.ShapeDtypeStruct((1, loads, channels, y_here, z_here, nx), f32),
            jax.ShapeDtypeStruct((yield_list.shape[0], strains), f32),
        ),
        in_specs=[hbm] * 7,
        out_specs=(vmem, vmem),
        scratch_shapes=[
            pltpu.SMEM(strain.shape, f32),
            pltpu.SMEM(tangent.shape, f32),
            pltpu.SMEM(yield_list.shape, jnp.int32),
            pltpu.SMEM(yield_list.shape, jnp.int32),
            pltpu.SMEM(stencil.shape, f32),
            pltpu.VMEM(polarization.shape[1:], f32),
            dma(6),
            pltpu.VMEM((groups, 8, 128), f32),
            pltpu.VMEM((loads, 128), f32),
            pltpu.VMEM((ny, nz, nx), jnp.int32),
            pltpu.VMEM((3, *polarization.shape[1:]), f32),
            pltpu.VMEM((ngz // CORES, channels, ny, z_here, nx), f32),
            pltpu.VMEM((count, channels, y_here, z_here, nx), f32),
            vector,
            pltpu.VMEM((3 * channels * nz, 3 * slot_rows), jnp.bfloat16),
            pltpu.VMEM((2, (ny + 2) * slot_rows, 2 * nx), jnp.bfloat16),
            vector,
            vector,
            cell, cell, cell, cell,
            pltpu.VMEM((CAP, 1, 128), f32),
            pltpu.VMEM((groups, CORES, CAP, 1, 128), f32),
            dma(groups), dma(groups), dma(count), dma(count),
            dma(3, channels), dma(3, channels),
            dma(ngz // CORES, ny), dma(ngz // CORES, ny),
            dma(count), dma(count),
            dma(ngy, ngz, y_here), dma(ngy, ngz, y_here),
            dma(ngy, ngz), dma(groups, CORES), dma(2 + y_here),
        ],
        compiler_params=pltpu.CompilerParams(
            collective_id=0, has_side_effects=True, vmem_limit_bytes=40 * 1024 * 1024
        ),
    )(*[
        pltpu.with_memory_space_constraint(argument, pltpu.HBM)
        for argument in (
            strain, tangent, yield_list, destination[:, 0], stencil, phase_map, polarization
        )
    ])
    return pl.pallas_call(
        deliver,
        out_shape=(
            jax.ShapeDtypeStruct(held_fields.shape, f32),
            jax.ShapeDtypeStruct(held_rows.shape, f32),
        ),
        in_specs=[vmem, vmem],
        out_specs=(hbm, hbm),
        scratch_shapes=[dma(2)],
        compiler_params=pltpu.CompilerParams(vmem_limit_bytes=4 * 1024 * 1024),
    )(held_fields, held_rows)


def body_for(mesh):
    def chosen(*arguments):
        strain, _, yield_list, _, phase_map, _, _ = arguments
        loads = lax.axis_size("rve") * CAP
        one_load_each = lax.axis_size("gy") == 2 and lax.axis_size("gz") == 2 * CORES
        tiled = phase_map.shape[2] == 8 and phase_map.shape[3] == 128 and loads == 8
        if one_load_each and tiled and yield_list.shape[0] <= 8:
            return fused_body(*arguments)
        return body(*arguments)

    return chosen


def solution(mesh):
    return jax.shard_map(
        body_for(mesh),
        mesh=mesh,
        in_specs=(
            P("rve", None),
            P("rve"),
            P("rve"),
            P("rve", None),
            P("rve", "gy", "gz", None),
            P("rve", None, None, "gy", "gz", None),
            P(),
        ),
        out_specs=(P("rve", None, None, "gy", "gz", None), P("rve", None)),
        check_vma=False,
    )
```

```python
import functools

import jax
import jax.numpy as jnp
from jax import lax
from jax.experimental import pallas as pl
from jax.experimental.pallas import tpu as pltpu
from jax.sharding import PartitionSpec as P

CAP = 2
CORES = 2
SKEWED = 1
PASSES = (16, 24)
SENT_ROWS = 2
SWEEPS = 6
MESH = pl.DeviceIdType.MESH
TANGENT, TARGET, RANK, LISTED = 6, 7, 8, 9


FULL_PRECISION = lax.Precision.HIGHEST
LOWER_BOUND = 0.05
UPPER_BOUND = 1.95


def padded(block, sides, width):
    for axis, dim in sides:
        count = lax.axis_size(axis)
        forward = [(i, i + 1) for i in range(count - 1)]
        forward.append((count - 1, 0))
        backward = [(target, source) for source, target in forward]
        low = lax.ppermute(
            lax.slice_in_dim(block, block.shape[dim] - width, None, axis=dim), axis, forward
        )
        high = lax.ppermute(lax.slice_in_dim(block, 0, width, axis=dim), axis, backward)
        block = jnp.concatenate([low, block, high], axis=dim)
    return block


def chebyshev_weights(sweep_count):
    centre_value = 0.5 * (UPPER_BOUND + LOWER_BOUND)
    half_width = 0.5 * (UPPER_BOUND - LOWER_BOUND)
    ratio_value = centre_value / half_width
    rho_before = 1.0 / ratio_value
    weights = []
    for sweep_index in range(1, sweep_count):
        rho_after = 1.0 / (2.0 * ratio_value - rho_before)
        weights.append((rho_after * rho_before, 2.0 * rho_after / half_width))
        rho_before = rho_after
    return (1.0 / centre_value, weights)


def skewed_order(rows, half, levels):
    def needed(level, row):
        steps = [(level, row)]
        if level:
            for shift in (-1, 0, 1):
                steps += needed(level - 1, (row + shift) % rows)
        return steps

    finals = []
    for away in range(rows // 2):
        finals += [(half + away) % rows, (half - 1 - away) % rows]
    finals = [row for pair in range(0, rows, 4) for row in finals[pair : pair + 4 : 2] + finals[pair + 1 : pair + 4 : 2]]
    placed = {}
    order = []
    while len(order) < rows * levels:
        choice = None
        for lag in (2, 1):
            for final in finals:
                for level, row in sorted(set(needed(levels - 1, final))):
                    inputs = needed(level, row)[1:]
                    ready = all(placed.get(step, rows * levels) <= len(order) - lag for step in inputs)
                    if choice is None and (level, row) not in placed and ready:
                        choice = (level, row)
        placed[choice] = len(order)
        order.append(choice)
    return order


def trim_margin(values_in, margin_have, margin_want, first_dim):
    excess = margin_have - margin_want
    values_in = lax.slice_in_dim(
        values_in, excess, values_in.shape[first_dim] - excess, axis=first_dim
    )
    return lax.slice_in_dim(
        values_in, excess, values_in.shape[first_dim + 1] - excess, axis=first_dim + 1
    )


def apply_stiffness(field_now, moduli, stencil):
    inner_y = field_now.shape[2] - 2
    inner_z = field_now.shape[3] - 2
    centre_mod = moduli[:, 1 : 1 + inner_y, 1 : 1 + inner_z, :]
    running = [None, None, None]
    for shift_y in (-1, 0, 1):
        for shift_z in (-1, 0, 1):
            shifted = field_now[
                :, :, 1 + shift_y : 1 + shift_y + inner_y, 1 + shift_z : 1 + shift_z + inner_z, :
            ]
            shifted_mod = moduli[
                :, 1 + shift_y : 1 + shift_y + inner_y, 1 + shift_z : 1 + shift_z + inner_z, :
            ]
            for shift_x in (-1, 0, 1):
                if shift_x != 0:
                    rolled = jnp.roll(shifted, -shift_x, axis=4)
                    rolled_mod = jnp.roll(shifted_mod, -shift_x, axis=3)
                else:
                    rolled = shifted
                    rolled_mod = shifted_mod
                offset_index = (shift_y + 1) * 9 + (shift_z + 1) * 3 + (shift_x + 1)
                edge_mod = 0.5 * (centre_mod + rolled_mod)
                weighted = [edge_mod * rolled[:, channel_in] for channel_in in range(3)]
                for channel_out in range(3):
                    mixed = stencil[channel_out, 0, offset_index] * weighted[0]
                    mixed = mixed + stencil[channel_out, 1, offset_index] * weighted[1]
                    mixed = mixed + stencil[channel_out, 2, offset_index] * weighted[2]
                    if running[channel_out] is None:
                        running[channel_out] = mixed
                    else:
                        running[channel_out] = running[channel_out] + mixed
    return jnp.stack(running, axis=1)


def body(strain, tangent, yield_list, destination, phase_map, polarization, stencil):
    groups = lax.axis_size("rve")
    rows_here = strain.shape[0]
    yield_count = yield_list.shape[0]
    picker = (jnp.arange(rows_here, dtype=jnp.int32)[None, :] == yield_list[:, None]).astype(
        jnp.float32
    )
    row_strain = jnp.dot(picker, strain, precision=FULL_PRECISION)
    row_tangent = jnp.dot(picker, tangent, precision=FULL_PRECISION)
    target = destination[:, 0]
    positions = jnp.arange(yield_count, dtype=jnp.int32)
    earlier = (target[:, None] == target[None, :]) & (positions[None, :] < positions[:, None])
    rank_in = jnp.sum(earlier.astype(jnp.int32), axis=1)
    group_ids = jnp.arange(groups, dtype=jnp.int32)
    slot_ids = jnp.arange(CAP, dtype=jnp.int32)
    onehot = (
        (target[None, None, :] == group_ids[:, None, None])
        & (rank_in[None, None, :] == slot_ids[None, :, None])
    ).astype(jnp.float32)
    packet = jnp.einsum("gci,ij->gcj", onehot, row_strain, precision=FULL_PRECISION)
    packet_tangent = (
        jnp.einsum("gci,i->gc", onehot, row_tangent, precision=FULL_PRECISION)
        + 1.0
        - jnp.sum(onehot, axis=2)
    )
    parcel = jnp.concatenate([packet, packet_tangent[:, :, None]], axis=2)
    arrived = lax.all_to_all(parcel, "rve", split_axis=0, concat_axis=0, tiled=True)
    slot_strain = arrived[:, :, :6].reshape(groups * CAP, 6)
    slot_tangent = arrived[:, :, 6].reshape(groups * CAP)
    phase_wide = padded(phase_map[0], (("gy", 0), ("gz", 1)), 2)
    moduli_wide = jnp.where(
        phase_wide[None] == 1, slot_tangent[:, None, None, None], jnp.float32(1.0)
    )
    moduli_core = trim_margin(moduli_wide, 2, 0, 1)
    moduli_one = trim_margin(moduli_wide, 2, 1, 1)
    polar_local = polarization[0]
    centre_diag = jnp.diagonal(stencil[:, :, 13])
    body_force = moduli_core[:, None] * jnp.einsum(
        "cjyzx,lj->lcyzx", polar_local, slot_strain, precision=FULL_PRECISION
    )
    inverse_diag = 1.0 / (centre_diag[None, :, None, None, None] * moduli_core[:, None])
    first_weight, weights = chebyshev_weights(SWEEPS)
    update = first_weight * (body_force * inverse_diag)
    field_now = update
    for old_weight, new_weight in weights:
        wrapped = padded(field_now, (("gy", 2), ("gz", 3)), 1)
        residual_now = body_force - apply_stiffness(wrapped, moduli_one, stencil)
        update = old_weight * update + new_weight * (residual_now * inverse_diag)
        field_now = field_now + update
    coupled = jnp.einsum(
        "cjyzx,lcyzx->lj", polar_local, moduli_core[:, None] * field_now, precision=FULL_PRECISION
    )
    partial_value = coupled + slot_strain * jnp.sum(moduli_core, axis=(1, 2, 3))[:, None]
    total_cells = (
        lax.axis_size("gy")
        * lax.axis_size("gz")
        * field_now.shape[2]
        * field_now.shape[3]
        * field_now.shape[4]
    )
    summed = lax.psum(partial_value, ("gy", "gz")) / total_cells
    returned = lax.all_to_all(
        summed.reshape(groups, CAP, 6), "rve", split_axis=0, concat_axis=0, tiled=True
    )
    stress_rows = jnp.einsum("gci,gcj->ij", onehot, returned, precision=FULL_PRECISION)
    return (field_now[None], stress_rows)


def kernel(
    groups, ngy, ngz,
    strain_hbm, tangent_hbm, yield_hbm, destination_hbm, stencil_hbm, phase_hbm, polar_hbm,
    fields, rows_out,
    strain, tangent, yield_list, destination, stencil, polar, load_sem,
    tables, slots, phase_all, polar_far, twin_field, force_out, force, matrix, spread, field_now, update,
    mod_mid, mod_low, mod_high, mod_inv, stress, totals,
    table_send, table_recv, phase_send, phase_recv, polar_send, polar_recv,
    twin_send, twin_recv, force_send, force_recv,
    field_send, field_recv, total_send, total_recv, own_sem,
):
    f32, bf16 = jnp.float32, jnp.bfloat16
    channels, strains = polar.shape[:2]
    y_here, z_here, nx = polar.shape[2:]
    ny, nz = y_here * ngy, z_here * ngz
    loaded = [
        pltpu.make_async_copy(source, held, load_sem.at[index])
        for index, (source, held) in enumerate(
            [
                (destination_hbm, destination), (yield_hbm, yield_list), (strain_hbm, strain),
                (tangent_hbm, tangent), (polar_hbm.at[0], polar), (stencil_hbm, stencil),
            ]
        )
    ]
    for copy in loaded:
        copy.start()
    wide = channels * nz
    slot_rows = 3 * wide
    depth = 3 * slot_rows
    listed = yield_list.shape[0]
    loads = groups * CAP
    my_r, my_y, my_z = lax.axis_index("rve"), lax.axis_index("gy"), lax.axis_index("gz")
    my_load = my_y * ngz + my_z

    def turned(base, step, count):
        return lax.rem(base + step + count, count)

    mates = [(dy, dz) for dy in list(range(1, ngy)) + [0] for dz in list(range(1, ngz)) + [0]]
    others = [mate for mate in mates if mate != (0, 0)]

    def mate_id(dy, dz):
        return {"gy": turned(my_y, dy, ngy), "gz": turned(my_z, dz, ngz)}

    def block(dy):
        y_at = -dy % ngy * y_here
        z_at = pl.multiple_of(my_z * z_here, 8)
        return pl.ds(y_at, y_here), pl.ds(z_at, z_here)

    barrier = pltpu.get_barrier_semaphore()
    for dy, dz in others:
        pl.semaphore_signal(barrier, inc=1, device_id=mate_id(dy, dz), device_id_type=MESH)
    for step in range(1, groups):
        pl.semaphore_signal(
            barrier, inc=1, device_id={"rve": turned(my_r, step, groups)}, device_id_type=MESH
        )

    for copy in loaded[:4]:
        copy.wait()
    row_ids = lax.broadcasted_iota(jnp.int32, (8, 128), 0)
    lane_ids = lax.broadcasted_iota(jnp.int32, (8, 128), 1)
    table = jnp.zeros((8, 128), f32)
    for i in range(listed):
        point, target = yield_list[i], destination[i]
        rank = jnp.int32(0)
        for k in range(i):
            rank = rank + jnp.where(destination[k] == target, 1, 0)
        values = [strain[point, j] for j in range(strains)]
        values += [tangent[point], target.astype(f32), rank.astype(f32), jnp.float32(1.0)]
        for j, value in enumerate(values):
            table = jnp.where((row_ids == i) & (lane_ids == j), value, table)
    tables[my_r] = table

    pl.semaphore_wait(barrier, len(others) + groups - 1)

    def table_copy(step, owner):
        return pltpu.make_async_remote_copy(
            src_ref=tables.at[my_r], dst_ref=tables.at[owner],
            send_sem=table_send.at[step], recv_sem=table_recv.at[step],
            device_id={"rve": turned(my_r, step, groups)}, device_id_type=MESH,
        )

    def phase_copy(index):
        to_y, to_z = others[index]
        y_at, z_at = block(to_y)
        return pltpu.make_async_remote_copy(
            src_ref=phase_hbm.at[0], dst_ref=phase_all.at[y_at, z_at],
            send_sem=phase_send.at[index], recv_sem=phase_recv.at[index],
            device_id=mate_id(to_y, to_z), device_id_type=MESH,
        )

    across, along, corner = (1, 0), (0, CORES), (1, CORES)
    twins = [across, along, corner]
    my_core = lax.rem(my_z, CORES)
    turn = 1 - 2 * my_core

    def polar_copy(index, c):
        return pltpu.make_async_remote_copy(
            src_ref=polar_hbm.at[0, c], dst_ref=polar_far.at[index, c],
            send_sem=polar_send.at[index, c], recv_sem=polar_recv.at[index, c],
            device_id=mate_id(*twins[index]), device_id_type=MESH,
        )

    def onward_copy(c):
        return pltpu.make_async_remote_copy(
            src_ref=polar_far.at[my_core, c], dst_ref=polar_far.at[2, c],
            send_sem=polar_send.at[2, c], recv_sem=polar_recv.at[2, c],
            device_id=mate_id(my_core, CORES * (1 - my_core)), device_id_type=MESH,
        )

    def send_polar(channels_now):
        for c in channels_now:
            for index in range(2):
                polar_copy(index, c).start()

    def pass_on(c):
        for index in range(2):
            polar_copy(index, c).wait_recv()
        onward_copy(c).start()

    for step in range(1, groups):
        table_copy(step, my_r).start()
    for index in range(len(others)):
        phase_copy(index).start()
    own_y, own_z = block(0)
    own_phase = pltpu.make_async_copy(phase_hbm.at[0], phase_all.at[own_y, own_z], own_sem.at[0])
    own_phase.start()
    send_polar(range(1))

    for step in range(1, groups):
        table_copy(step, turned(my_r, -step, groups)).wait_recv()
    for source in range(groups):
        heard = tables[source]
        named = (heard[:, TARGET : TARGET + 1] == my_r.astype(f32)) & (
            heard[:, LISTED : LISTED + 1] == 1.0
        )
        for rank in range(CAP):
            chosen = named & (heard[:, RANK : RANK + 1] == float(rank))
            line = jnp.sum(jnp.where(chosen, heard, 0.0), axis=0, keepdims=True)
            missing = 1.0 - line[:, LISTED : LISTED + 1]
            line = line + jnp.where(lane_ids[:1] == TANGENT, missing, 0.0)
            at = source * CAP + rank
            slots[at : at + 1, :] = line

    loaded[4].wait()

    def slot_value(load, index):
        return jnp.broadcast_to(slots[pl.ds(load, 1), :][:, index : index + 1], (8, 128))

    def force_copy(index):
        y_at, z_at = block(others[index][0])
        return pltpu.make_async_remote_copy(
            src_ref=force_out.at[index], dst_ref=force.at[:, y_at, z_at],
            send_sem=force_send.at[index], recv_sem=force_recv.at[index],
            device_id=mate_id(*others[index]), device_id_type=MESH,
        )

    for index, (dy, dz) in enumerate(mates):
        load = turned(my_y, dy, ngy) * ngz + turned(my_z, dz, ngz)
        strain_of = [slot_value(load, j) for j in range(strains)]
        for c in range(channels):
            for y in range(y_here):
                value = polar[c, 0, y] * strain_of[0]
                for j in range(1, strains):
                    value = value + polar[c, j, y] * strain_of[j]
                if (dy, dz) == (0, 0):
                    force[c, y, own_z, :] = value
                else:
                    force_out[index, c, y] = value
        if (dy, dz) != (0, 0):
            force_copy(index).start()

    send_polar(range(1, channels))
    loaded[5].wait()
    column = lax.broadcasted_iota(jnp.int32, (1, depth), 1)
    column_y = column // slot_rows
    column_kind = lax.rem(column, slot_rows) // wide
    column_d = lax.rem(column, wide) // nz
    picks = [[(column_y == dy) & (column_d == d) for d in range(channels)] for dy in range(3)]
    z_row = lax.broadcasted_iota(jnp.int32, (nz, depth), 0)
    z_column = lax.rem(lax.broadcasted_iota(jnp.int32, (nz, depth), 1), nz)
    bands = [z_column == lax.rem(z_row + dz - 1 + nz, nz) for dz in range(3)]
    is_low = jnp.broadcast_to(column_kind, (nz, depth)) == 1
    for dx in range(3):
        for c in range(channels):
            values = jnp.zeros((nz, depth), f32)
            for dz in range(3):
                line = jnp.zeros((1, depth), f32)
                for dy in range(3):
                    for d in range(channels):
                        line = jnp.where(
                            picks[dy][d], 0.5 * stencil[c, d, dy * 9 + dz * 3 + dx], line
                        )
                values = values + jnp.where(bands[dz], line, 0.0)
            high = values.astype(bf16).astype(f32)
            low = values - high
            at = (dx * channels + c) * nz
            matrix[at : at + nz, :] = jnp.where(is_low, low, high).astype(bf16)

    for index, (dy, dz) in enumerate(others):
        phase_copy(index).wait_recv()
    own_phase.wait()
    tangent_row = slots[pl.ds(my_load, 1), :][:, TANGENT : TANGENT + 1]
    my_tangent = jnp.broadcast_to(tangent_row, (nz, nx))
    inverse_tangent = 1.0 / my_tangent
    for y in range(ny):
        second = phase_all[y] == 1
        mod = jnp.where(second, my_tangent, 1.0)
        mod_mid[y] = mod
        mod_low[y] = pltpu.roll(mod, nx - 1, 1)
        mod_high[y] = pltpu.roll(mod, 1, 1)
        mod_inv[y] = jnp.where(second, inverse_tangent, 1.0)
    ones = jnp.ones((nz, nx), f32)
    inverse_centre = [1.0 / (ones * stencil[c, c, 13]) for c in range(channels)]

    def put(buffer, y, c, value):
        both = jnp.concatenate([value, value * mod_mid[y]], axis=1)
        high = both.astype(bf16)
        low = (both - high.astype(f32)).astype(bf16)
        places = [y + 1] + ([ny + 1] if y == 0 else []) + ([0] if y == ny - 1 else [])
        for place in places:
            at = place * slot_rows + c * nz
            spread[buffer, at : at + nz, :] = high
            spread[buffer, at + wide : at + wide + nz, :] = high
            spread[buffer, at + 2 * wide : at + 2 * wide + nz, :] = low

    first_weight, weights = chebyshev_weights(SWEEPS)
    quarters = (ngz // CORES, CORES, z_here, nx)
    for y in list(range(y_here, ny)) + list(range(y_here)):
        if y % y_here == 0:
            for index, (dy, dz) in enumerate(others):
                if dy == y // y_here:
                    force_copy(index).wait_recv()
        for c in range(channels):
            value = first_weight * (force[c, y] * inverse_centre[c])
            update[c, y] = value
            field_now[c, y] = value.reshape(quarters)
            put(0, y, c, value)

    pass_on(0)

    def row_product(buffer, y):
        at = y * slot_rows
        return jnp.dot(
            matrix[...], spread[buffer, pl.ds(at, depth), :], preferred_element_type=f32
        )

    def finish_row(product, buffer, y, old_weight, new_weight, last):
        for c in range(channels):
            parts = []
            for dx, mod in enumerate((mod_low, mod_mid, mod_high)):
                row = (dx * channels + c) * nz
                parts.append(
                    mod[y] * product[row : row + nz, :nx] + product[row : row + nz, nx:]
                )
            stiff = parts[1] + pltpu.roll(parts[0], 1, 1) + pltpu.roll(parts[2], nx - 1, 1)
            residual = (force[c, y] - stiff * mod_inv[y]) * inverse_centre[c]
            step = old_weight * update[c, y] + new_weight * residual
            value = field_now[c, y].reshape(nz, nx) + step
            field_now[c, y] = value.reshape(quarters)
            if not last:
                update[c, y] = step
                put(1 - buffer, y, c, value)

    def sweep(k, carry):
        old_weight, new_weight = jnp.float32(weights[0][0]), jnp.float32(weights[0][1])
        for position in range(1, plain):
            old_weight = jnp.where(k == position, weights[position][0], old_weight)
            new_weight = jnp.where(k == position, weights[position][1], new_weight)
        buffer = lax.rem(k, 2)
        product = row_product(buffer, 0)
        for y in range(ny):
            later = row_product(buffer, y + 1) if y + 1 < ny else None
            finish_row(product, buffer, y, old_weight, new_weight, False)
            product = later
        for c, after in enumerate(PASSES):
            if after % ny == 0 and after <= plain * ny:
                pl.when(k == after // ny - 1)(functools.partial(pass_on, c + 1))
        return carry

    plain = len(weights) - SKEWED
    lax.fori_loop(0, plain, sweep, 0)

    sides = [(dy, dz, dz) for dy in range(1, ngy) for dz in range(ngz)]
    sides += [(0, 1, CORES), (0, 2, CORES + turn)]

    groups_here = y_here // SENT_ROWS

    def rows_of(group):
        return pl.ds(group * SENT_ROWS, SENT_ROWS)

    def field_copy(dy, place, dz, group, load):
        to_y, to_z = turned(my_y, dy, ngy), turned(my_z, dz, ngz)
        return pltpu.make_async_remote_copy(
            src_ref=field_now.at[
                :, rows_of(dy * groups_here + group), to_z // CORES, lax.rem(to_z, CORES)
            ],
            dst_ref=fields.at[0, load, :, rows_of(group)],
            send_sem=field_send.at[dy, place, group], recv_sem=field_recv.at[dy, place, group],
            device_id={"gy": to_y, "gz": to_z}, device_id_type=MESH,
        )

    def twin_copy(group):
        return pltpu.make_async_remote_copy(
            src_ref=field_now.at[:, rows_of(group), :, 1 - my_core],
            dst_ref=twin_field.at[:, rows_of(group)],
            send_sem=twin_send.at[group], recv_sem=twin_recv.at[group],
            device_id=mate_id(0, turn), device_id_type=MESH,
        )

    def own_field(group):
        return pltpu.make_async_copy(
            field_now.at[:, rows_of(group), my_z // CORES, my_core],
            fields.at[0, my_load, :, rows_of(group)],
            own_sem.at[2 + group],
        )

    order = skewed_order(ny, y_here, SKEWED)
    product = row_product(plain % 2, order[0][1])
    for place, (level, row) in enumerate(order):
        later = None
        if place + 1 < len(order):
            later = row_product((plain + order[place + 1][0]) % 2, order[place + 1][1])
        last = level == SKEWED - 1
        finish_row(product, (plain + level) % 2, row, *weights[plain + level], last)
        product = later
        group = row // SENT_ROWS
        waiting = [step for step in order[place + 1 :] if step in [
            (SKEWED - 1, group * SENT_ROWS + other) for other in range(SENT_ROWS)
        ]]
        if last and not waiting:
            twin_copy(group).start()
            for side, where, dz in sides:
                if side == group // groups_here:
                    field_copy(side, where, dz, group % groups_here, my_load).start()
            if group < groups_here:
                own_field(group).start()
        for c, after in enumerate(PASSES):
            if after == plain * ny + place + 1 and after > plain * ny:
                pass_on(c + 1)

    for group in range(ngy * groups_here):
        twin_copy(group).wait_recv()
    for c in range(1, channels + 1):
        if c < channels:
            polar_copy(2, c).wait_recv()
        else:
            polar_copy(2, 0).wait_recv()
    twin_load = my_load + turn
    slopes = [slot_value(my_load, TANGENT), slot_value(twin_load, TANGENT)]
    totals_of = [[jnp.zeros((z_here, nx), f32) for _ in range(strains)] for _ in range(2)]
    counted = jnp.zeros((z_here, nx), f32)
    for index, (dy, dz) in enumerate([(0, 0)] + twins):
        part = lax.rem(my_z // CORES + dz // CORES, ngz // CORES)
        for y in range(y_here):
            row = dy * y_here + y
            z_at = pl.ds(pl.multiple_of((CORES * part + my_core) * z_here, 8), z_here)
            second = phase_all[row, z_at, :] == 1
            counted = counted + jnp.where(second, 1.0, 0.0)
            mods = [jnp.where(second, slope, 1.0) for slope in slopes]
            for c in range(channels):
                theirs = twin_field[c, row, part]
                if index == 0:
                    fields[0, twin_load, c, y] = theirs
                fluxes = [mods[0] * field_now[c, row, part, my_core], mods[1] * theirs]
                for j in range(strains):
                    weight = polar[c, j, y] if index == 0 else polar_far[index - 1, c, j, y]
                    for which in range(2):
                        totals_of[which][j] = totals_of[which][j] + weight * fluxes[which]

    def whole_sum(values):
        return jnp.sum(jnp.sum(values, axis=0, keepdims=True), axis=1, keepdims=True)

    second_count = whole_sum(counted)
    for which, load in enumerate((my_load, twin_load)):
        line = slots[pl.ds(load, 1), :]
        mod_sum = second_count * line[:, TANGENT : TANGENT + 1] + (
            float(len(twins) + 1) * y_here * z_here * nx - second_count
        )
        line = line * mod_sum
        for j in range(strains):
            line = line + jnp.where(lane_ids[:1] == j, whole_sum(totals_of[which][j]), 0.0)
        stress[lax.rem(load, CAP)] = line * (1.0 / (ny * nz * nx))

    my_macro = my_load // CAP

    def total_copy(dy, dz):
        return pltpu.make_async_remote_copy(
            src_ref=stress, dst_ref=totals.at[my_r, my_core],
            send_sem=total_send.at[dy, dz], recv_sem=total_recv.at[my_r, my_core],
            device_id={"rve": my_macro, **mate_id(dy, dz)}, device_id_type=MESH,
        )

    def total_arrival(group, core):
        return pltpu.make_async_remote_copy(
            src_ref=stress, dst_ref=totals.at[group, core],
            send_sem=total_send.at[0, 0], recv_sem=total_recv.at[group, core],
            device_id={"rve": turned(my_r, 1, groups)}, device_id_type=MESH,
        )

    for dy, dz in others:
        total_copy(dy, dz).start()

    @pl.when(my_macro != my_r)
    def _():
        total_copy(0, 0).start()

    @pl.when(my_macro == my_r)
    def _():
        totals[my_r, my_core] = stress[...]

    for group in range(groups):
        for core in range(CORES):
            @pl.when((my_r != group) | (my_macro != group) | (my_core != core))
            def _():
                total_arrival(group, core).wait_recv()

    mine = tables[my_r]
    answer = jnp.zeros((8, 128), f32)
    for group in range(groups):
        for rank in range(CAP):
            chosen = (mine[:, TARGET : TARGET + 1] == float(group)) & (
                mine[:, RANK : RANK + 1] == float(rank)
            )
            line = totals[group, 0, rank]
            for core in range(1, CORES):
                line = line + totals[group, core, rank]
            answer = answer + jnp.where(chosen, line, 0.0)
    rows_out[...] = answer[:listed, :strains]

    @pl.when(my_macro != my_r)
    def _():
        total_copy(0, 0).wait_send()

    for c in range(channels):
        for index in range(2):
            polar_copy(index, c).wait_send()
        onward_copy(c).wait_send()
    for group in range(groups_here):
        own_field(group).wait()
    for step in range(1, groups):
        table_copy(step, my_r).wait_send()
    for index, (dy, dz) in enumerate(others):
        phase_copy(index).wait_send()
        force_copy(index).wait_send()
        total_copy(dy, dz).wait_send()
    for dy, where, dz in sides:
        load = turned(my_y, -dy, ngy) * ngz + turned(my_z, -dz, ngz)
        for group in range(groups_here):
            field_copy(dy, where, dz, group, my_load).wait_send()
            field_copy(dy, where, dz, group, load).wait_recv()
    for group in range(ngy * groups_here):
        twin_copy(group).wait_send()


def deliver(held_fields, held_rows, fields, rows_out, sem):
    copies = [
        pltpu.make_async_copy(held_fields, fields, sem.at[0]),
        pltpu.make_async_copy(held_rows, rows_out, sem.at[1]),
    ]
    for copy in copies:
        copy.start()
    for copy in copies:
        copy.wait()


def fused_body(strain, tangent, yield_list, destination, phase_map, polarization, stencil):
    groups, ngy, ngz = (lax.axis_size(name) for name in ("rve", "gy", "gz"))
    channels = polarization.shape[1]
    strains = polarization.shape[2]
    y_here, z_here, nx = polarization.shape[3:]
    ny, nz = y_here * ngy, z_here * ngz
    loads = groups * CAP
    count = ngy * ngz
    f32 = jnp.float32
    slot_rows = 3 * channels * nz
    vmem = pl.BlockSpec(memory_space=pltpu.VMEM)
    hbm = pl.BlockSpec(memory_space=pltpu.HBM)
    cell = pltpu.VMEM((ny, nz, nx), f32)
    vector = pltpu.VMEM((channels, ny, nz, nx), f32)

    def dma(*shape):
        return pltpu.SemaphoreType.DMA(shape)

    held_fields, held_rows = pl.pallas_call(
        functools.partial(kernel, groups, ngy, ngz),
        out_shape=(
            jax.ShapeDtypeStruct((1, loads, channels, y_here, z_here, nx), f32),
            jax.ShapeDtypeStruct((yield_list.shape[0], strains), f32),
        ),
        in_specs=[hbm] * 7,
        out_specs=(vmem, vmem),
        scratch_shapes=[
            pltpu.SMEM(strain.shape, f32),
            pltpu.SMEM(tangent.shape, f32),
            pltpu.SMEM(yield_list.shape, jnp.int32),
            pltpu.SMEM(yield_list.shape, jnp.int32),
            pltpu.SMEM(stencil.shape, f32),
            pltpu.VMEM(polarization.shape[1:], f32),
            dma(6),
            pltpu.VMEM((groups, 8, 128), f32),
            pltpu.VMEM((loads, 128), f32),
            pltpu.VMEM((ny, nz, nx), jnp.int32),
            pltpu.VMEM((3, *polarization.shape[1:]), f32),
            pltpu.VMEM((channels, ny, ngz // CORES, z_here, nx), f32),
            pltpu.VMEM((count, channels, y_here, z_here, nx), f32),
            vector,
            pltpu.VMEM((3 * channels * nz, 3 * slot_rows), jnp.bfloat16),
            pltpu.VMEM((2, (ny + 2) * slot_rows, 2 * nx), jnp.bfloat16),
            pltpu.VMEM((channels, ny, ngz // CORES, CORES, z_here, nx), f32),
            vector,
            cell, cell, cell, cell,
            pltpu.VMEM((CAP, 1, 128), f32),
            pltpu.VMEM((groups, CORES, CAP, 1, 128), f32),
            dma(groups), dma(groups), dma(count), dma(count),
            dma(3, channels), dma(3, channels),
            dma(ny), dma(ny),
            dma(count), dma(count),
            dma(ngy, ngz, y_here), dma(ngy, ngz, y_here),
            dma(ngy, ngz), dma(groups, CORES), dma(2 + y_here),
        ],
        compiler_params=pltpu.CompilerParams(
            collective_id=0, has_side_effects=True, vmem_limit_bytes=40 * 1024 * 1024
        ),
    )(*[
        pltpu.with_memory_space_constraint(argument, pltpu.HBM)
        for argument in (
            strain, tangent, yield_list, destination[:, 0], stencil, phase_map, polarization
        )
    ])
    return pl.pallas_call(
        deliver,
        out_shape=(
            jax.ShapeDtypeStruct(held_fields.shape, f32),
            jax.ShapeDtypeStruct(held_rows.shape, f32),
        ),
        in_specs=[vmem, vmem],
        out_specs=(hbm, hbm),
        scratch_shapes=[dma(2)],
        compiler_params=pltpu.CompilerParams(vmem_limit_bytes=4 * 1024 * 1024),
    )(held_fields, held_rows)


def body_for(mesh):
    def chosen(*arguments):
        strain, _, yield_list, _, phase_map, _, _ = arguments
        loads = lax.axis_size("rve") * CAP
        one_load_each = lax.axis_size("gy") == 2 and lax.axis_size("gz") == 2 * CORES
        tiled = phase_map.shape[2] == 8 and phase_map.shape[3] == 128 and loads == 8
        if one_load_each and tiled and yield_list.shape[0] <= 8:
            return fused_body(*arguments)
        return body(*arguments)

    return chosen


def solution(mesh):
    return jax.shard_map(
        body_for(mesh),
        mesh=mesh,
        in_specs=(
            P("rve", None),
            P("rve"),
            P("rve"),
            P("rve", None),
            P("rve", "gy", "gz", None),
            P("rve", None, None, "gy", "gz", None),
            P(),
        ),
        out_specs=(P("rve", None, None, "gy", "gz", None), P("rve", None)),
        check_vma=False,
    )
```

```python
import functools

import jax
import jax.numpy as jnp
from jax import lax
from jax.experimental import pallas as pl
from jax.experimental.pallas import tpu as pltpu
from jax.sharding import PartitionSpec as P

CAP = 2
CORES = 2
SKEWED = 1
PASSES = (16, 24)
SENT_ROWS = 2
SWEEPS = 6
MESH = pl.DeviceIdType.MESH
TANGENT, TARGET, RANK, LISTED = 6, 7, 8, 9


FULL_PRECISION = lax.Precision.HIGHEST
LOWER_BOUND = 0.05
UPPER_BOUND = 1.95


def padded(block, sides, width):
    for axis, dim in sides:
        count = lax.axis_size(axis)
        forward = [(i, i + 1) for i in range(count - 1)]
        forward.append((count - 1, 0))
        backward = [(target, source) for source, target in forward]
        low = lax.ppermute(
            lax.slice_in_dim(block, block.shape[dim] - width, None, axis=dim), axis, forward
        )
        high = lax.ppermute(lax.slice_in_dim(block, 0, width, axis=dim), axis, backward)
        block = jnp.concatenate([low, block, high], axis=dim)
    return block


def chebyshev_weights(sweep_count):
    centre_value = 0.5 * (UPPER_BOUND + LOWER_BOUND)
    half_width = 0.5 * (UPPER_BOUND - LOWER_BOUND)
    ratio_value = centre_value / half_width
    rho_before = 1.0 / ratio_value
    weights = []
    for sweep_index in range(1, sweep_count):
        rho_after = 1.0 / (2.0 * ratio_value - rho_before)
        weights.append((rho_after * rho_before, 2.0 * rho_after / half_width))
        rho_before = rho_after
    return (1.0 / centre_value, weights)


def skewed_order(rows, half, levels):
    def needed(level, row):
        steps = [(level, row)]
        if level:
            for shift in (-1, 0, 1):
                steps += needed(level - 1, (row + shift) % rows)
        return steps

    finals = []
    for away in range(rows // 2):
        finals += [(half + away) % rows, (half - 1 - away) % rows]
    finals = [row for pair in range(0, rows, 4) for row in finals[pair : pair + 4 : 2] + finals[pair + 1 : pair + 4 : 2]]
    placed = {}
    order = []
    while len(order) < rows * levels:
        choice = None
        for lag in (2, 1):
            for final in finals:
                for level, row in sorted(set(needed(levels - 1, final))):
                    inputs = needed(level, row)[1:]
                    ready = all(placed.get(step, rows * levels) <= len(order) - lag for step in inputs)
                    if choice is None and (level, row) not in placed and ready:
                        choice = (level, row)
        placed[choice] = len(order)
        order.append(choice)
    return order


def trim_margin(values_in, margin_have, margin_want, first_dim):
    excess = margin_have - margin_want
    values_in = lax.slice_in_dim(
        values_in, excess, values_in.shape[first_dim] - excess, axis=first_dim
    )
    return lax.slice_in_dim(
        values_in, excess, values_in.shape[first_dim + 1] - excess, axis=first_dim + 1
    )


def apply_stiffness(field_now, moduli, stencil):
    inner_y = field_now.shape[2] - 2
    inner_z = field_now.shape[3] - 2
    centre_mod = moduli[:, 1 : 1 + inner_y, 1 : 1 + inner_z, :]
    running = [None, None, None]
    for shift_y in (-1, 0, 1):
        for shift_z in (-1, 0, 1):
            shifted = field_now[
                :, :, 1 + shift_y : 1 + shift_y + inner_y, 1 + shift_z : 1 + shift_z + inner_z, :
            ]
            shifted_mod = moduli[
                :, 1 + shift_y : 1 + shift_y + inner_y, 1 + shift_z : 1 + shift_z + inner_z, :
            ]
            for shift_x in (-1, 0, 1):
                if shift_x != 0:
                    rolled = jnp.roll(shifted, -shift_x, axis=4)
                    rolled_mod = jnp.roll(shifted_mod, -shift_x, axis=3)
                else:
                    rolled = shifted
                    rolled_mod = shifted_mod
                offset_index = (shift_y + 1) * 9 + (shift_z + 1) * 3 + (shift_x + 1)
                edge_mod = 0.5 * (centre_mod + rolled_mod)
                weighted = [edge_mod * rolled[:, channel_in] for channel_in in range(3)]
                for channel_out in range(3):
                    mixed = stencil[channel_out, 0, offset_index] * weighted[0]
                    mixed = mixed + stencil[channel_out, 1, offset_index] * weighted[1]
                    mixed = mixed + stencil[channel_out, 2, offset_index] * weighted[2]
                    if running[channel_out] is None:
                        running[channel_out] = mixed
                    else:
                        running[channel_out] = running[channel_out] + mixed
    return jnp.stack(running, axis=1)


def body(strain, tangent, yield_list, destination, phase_map, polarization, stencil):
    groups = lax.axis_size("rve")
    rows_here = strain.shape[0]
    yield_count = yield_list.shape[0]
    picker = (jnp.arange(rows_here, dtype=jnp.int32)[None, :] == yield_list[:, None]).astype(
        jnp.float32
    )
    row_strain = jnp.dot(picker, strain, precision=FULL_PRECISION)
    row_tangent = jnp.dot(picker, tangent, precision=FULL_PRECISION)
    target = destination[:, 0]
    positions = jnp.arange(yield_count, dtype=jnp.int32)
    earlier = (target[:, None] == target[None, :]) & (positions[None, :] < positions[:, None])
    rank_in = jnp.sum(earlier.astype(jnp.int32), axis=1)
    group_ids = jnp.arange(groups, dtype=jnp.int32)
    slot_ids = jnp.arange(CAP, dtype=jnp.int32)
    onehot = (
        (target[None, None, :] == group_ids[:, None, None])
        & (rank_in[None, None, :] == slot_ids[None, :, None])
    ).astype(jnp.float32)
    packet = jnp.einsum("gci,ij->gcj", onehot, row_strain, precision=FULL_PRECISION)
    packet_tangent = (
        jnp.einsum("gci,i->gc", onehot, row_tangent, precision=FULL_PRECISION)
        + 1.0
        - jnp.sum(onehot, axis=2)
    )
    parcel = jnp.concatenate([packet, packet_tangent[:, :, None]], axis=2)
    arrived = lax.all_to_all(parcel, "rve", split_axis=0, concat_axis=0, tiled=True)
    slot_strain = arrived[:, :, :6].reshape(groups * CAP, 6)
    slot_tangent = arrived[:, :, 6].reshape(groups * CAP)
    phase_wide = padded(phase_map[0], (("gy", 0), ("gz", 1)), 2)
    moduli_wide = jnp.where(
        phase_wide[None] == 1, slot_tangent[:, None, None, None], jnp.float32(1.0)
    )
    moduli_core = trim_margin(moduli_wide, 2, 0, 1)
    moduli_one = trim_margin(moduli_wide, 2, 1, 1)
    polar_local = polarization[0]
    centre_diag = jnp.diagonal(stencil[:, :, 13])
    body_force = moduli_core[:, None] * jnp.einsum(
        "cjyzx,lj->lcyzx", polar_local, slot_strain, precision=FULL_PRECISION
    )
    inverse_diag = 1.0 / (centre_diag[None, :, None, None, None] * moduli_core[:, None])
    first_weight, weights = chebyshev_weights(SWEEPS)
    update = first_weight * (body_force * inverse_diag)
    field_now = update
    for old_weight, new_weight in weights:
        wrapped = padded(field_now, (("gy", 2), ("gz", 3)), 1)
        residual_now = body_force - apply_stiffness(wrapped, moduli_one, stencil)
        update = old_weight * update + new_weight * (residual_now * inverse_diag)
        field_now = field_now + update
    coupled = jnp.einsum(
        "cjyzx,lcyzx->lj", polar_local, moduli_core[:, None] * field_now, precision=FULL_PRECISION
    )
    partial_value = coupled + slot_strain * jnp.sum(moduli_core, axis=(1, 2, 3))[:, None]
    total_cells = (
        lax.axis_size("gy")
        * lax.axis_size("gz")
        * field_now.shape[2]
        * field_now.shape[3]
        * field_now.shape[4]
    )
    summed = lax.psum(partial_value, ("gy", "gz")) / total_cells
    returned = lax.all_to_all(
        summed.reshape(groups, CAP, 6), "rve", split_axis=0, concat_axis=0, tiled=True
    )
    stress_rows = jnp.einsum("gci,gcj->ij", onehot, returned, precision=FULL_PRECISION)
    return (field_now[None], stress_rows)


def kernel(
    groups, ngy, ngz,
    strain_hbm, tangent_hbm, yield_hbm, destination_hbm, stencil_hbm, phase_hbm, polar_hbm,
    fields, rows_out,
    strain, tangent, yield_list, destination, stencil, polar, load_sem,
    tables, slots, phase_all, polar_far, twin_field, force_out, force, matrix, spread, field_now, update,
    mod_mid, mod_low, mod_high, mod_inv, stress, totals,
    table_send, table_recv, phase_send, phase_recv, polar_send, polar_recv,
    twin_send, twin_recv, force_send, force_recv,
    field_send, field_recv, total_send, total_recv, own_sem,
):
    f32, bf16 = jnp.float32, jnp.bfloat16
    channels, strains = polar.shape[:2]
    y_here, z_here, nx = polar.shape[2:]
    ny, nz = y_here * ngy, z_here * ngz
    loaded = [
        pltpu.make_async_copy(source, held, load_sem.at[index])
        for index, (source, held) in enumerate(
            [
                (destination_hbm, destination), (yield_hbm, yield_list), (strain_hbm, strain),
                (tangent_hbm, tangent), (polar_hbm.at[0], polar), (stencil_hbm, stencil),
            ]
        )
    ]
    wide = channels * nz
    slot_rows = 3 * wide
    depth = 3 * slot_rows
    listed = yield_list.shape[0]
    loads = groups * CAP
    my_r, my_y, my_z = lax.axis_index("rve"), lax.axis_index("gy"), lax.axis_index("gz")
    my_load = my_y * ngz + my_z

    def turned(base, step, count):
        return lax.rem(base + step + count, count)

    mates = [(dy, dz) for dy in list(range(1, ngy)) + [0] for dz in list(range(1, ngz)) + [0]]
    others = [mate for mate in mates if mate != (0, 0)]

    def mate_id(dy, dz):
        return {"gy": turned(my_y, dy, ngy), "gz": turned(my_z, dz, ngz)}

    def block(dy):
        y_at = -dy % ngy * y_here
        z_at = pl.multiple_of(my_z * z_here, 8)
        return pl.ds(y_at, y_here), pl.ds(z_at, z_here)

    barrier = pltpu.get_barrier_semaphore()
    for step in range(1, groups):
        pl.semaphore_signal(
            barrier, inc=1, device_id={"rve": turned(my_r, step, groups)}, device_id_type=MESH
        )
    for copy in loaded[:4]:
        copy.start()
    for dy, dz in others:
        pl.semaphore_signal(barrier, inc=1, device_id=mate_id(dy, dz), device_id_type=MESH)
    for copy in loaded[4:]:
        copy.start()
    for copy in loaded[:4]:
        copy.wait()
    row_ids = lax.broadcasted_iota(jnp.int32, (8, 128), 0)
    lane_ids = lax.broadcasted_iota(jnp.int32, (8, 128), 1)
    table = jnp.zeros((8, 128), f32)
    for i in range(listed):
        point, target = yield_list[i], destination[i]
        rank = jnp.int32(0)
        for k in range(i):
            rank = rank + jnp.where(destination[k] == target, 1, 0)
        values = [strain[point, j] for j in range(strains)]
        values += [tangent[point], target.astype(f32), rank.astype(f32), jnp.float32(1.0)]
        for j, value in enumerate(values):
            table = jnp.where((row_ids == i) & (lane_ids == j), value, table)
    tables[my_r] = table

    pl.semaphore_wait(barrier, len(others) + groups - 1)

    def table_copy(step, owner):
        return pltpu.make_async_remote_copy(
            src_ref=tables.at[my_r], dst_ref=tables.at[owner],
            send_sem=table_send.at[step], recv_sem=table_recv.at[step],
            device_id={"rve": turned(my_r, step, groups)}, device_id_type=MESH,
        )

    def phase_copy(index):
        to_y, to_z = others[index]
        y_at, z_at = block(to_y)
        return pltpu.make_async_remote_copy(
            src_ref=phase_hbm.at[0], dst_ref=phase_all.at[y_at, z_at],
            send_sem=phase_send.at[index], recv_sem=phase_recv.at[index],
            device_id=mate_id(to_y, to_z), device_id_type=MESH,
        )

    across, along, corner = (1, 0), (0, CORES), (1, CORES)
    twins = [across, along, corner]
    my_core = lax.rem(my_z, CORES)
    turn = 1 - 2 * my_core

    def polar_copy(index, c):
        return pltpu.make_async_remote_copy(
            src_ref=polar_hbm.at[0, c], dst_ref=polar_far.at[index, c],
            send_sem=polar_send.at[index, c], recv_sem=polar_recv.at[index, c],
            device_id=mate_id(*twins[index]), device_id_type=MESH,
        )

    def polar_arrival(index, c):
        return pltpu.make_async_remote_copy(
            src_ref=polar_hbm.at[0, c], dst_ref=polar_far.at[index, c],
            send_sem=polar_send.at[index, c], recv_sem=polar_recv.at[index, c],
            device_id=mate_id(0, turn), device_id_type=MESH,
        )

    def onward_copy(c):
        return pltpu.make_async_remote_copy(
            src_ref=polar_far.at[my_core, c], dst_ref=polar_far.at[2, c],
            send_sem=polar_send.at[2, c], recv_sem=polar_recv.at[2, c],
            device_id=mate_id(my_core, CORES * (1 - my_core)), device_id_type=MESH,
        )

    def send_polar(channels_now):
        for c in channels_now:
            for index in range(2):
                polar_copy(index, c).start()

    def pass_on(c):
        polar_arrival(my_core, c).wait_recv()
        onward_copy(c).start()

    for step in range(1, groups):
        table_copy(step, my_r).start()
    for index in range(len(others)):
        phase_copy(index).start()
    own_y, own_z = block(0)
    own_phase = pltpu.make_async_copy(phase_hbm.at[0], phase_all.at[own_y, own_z], own_sem.at[0])
    own_phase.start()
    send_polar(range(1))

    for step in range(1, groups):
        table_copy(step, turned(my_r, -step, groups)).wait_recv()
    for source in range(groups):
        heard = tables[source]
        named = (heard[:, TARGET : TARGET + 1] == my_r.astype(f32)) & (
            heard[:, LISTED : LISTED + 1] == 1.0
        )
        for rank in range(CAP):
            chosen = named & (heard[:, RANK : RANK + 1] == float(rank))
            line = jnp.sum(jnp.where(chosen, heard, 0.0), axis=0, keepdims=True)
            missing = 1.0 - line[:, LISTED : LISTED + 1]
            line = line + jnp.where(lane_ids[:1] == TANGENT, missing, 0.0)
            at = source * CAP + rank
            slots[at : at + 1, :] = line

    loaded[4].wait()

    def slot_value(load, index):
        return jnp.broadcast_to(slots[pl.ds(load, 1), :][:, index : index + 1], (8, 128))

    def force_copy(index):
        y_at, z_at = block(others[index][0])
        return pltpu.make_async_remote_copy(
            src_ref=force_out.at[index], dst_ref=force.at[:, y_at, z_at],
            send_sem=force_send.at[index], recv_sem=force_recv.at[index],
            device_id=mate_id(*others[index]), device_id_type=MESH,
        )

    for index, (dy, dz) in enumerate(mates):
        load = turned(my_y, dy, ngy) * ngz + turned(my_z, dz, ngz)
        strain_of = [slot_value(load, j) for j in range(strains)]
        for c in range(channels):
            for y in range(y_here):
                value = polar[c, 0, y] * strain_of[0]
                for j in range(1, strains):
                    value = value + polar[c, j, y] * strain_of[j]
                if (dy, dz) == (0, 0):
                    force[c, y, own_z, :] = value
                else:
                    force_out[index, c, y] = value
        if (dy, dz) != (0, 0):
            force_copy(index).start()

    send_polar(range(1, channels))
    loaded[5].wait()
    column = lax.broadcasted_iota(jnp.int32, (1, depth), 1)
    column_y = column // slot_rows
    column_kind = lax.rem(column, slot_rows) // wide
    column_d = lax.rem(column, wide) // nz
    picks = [[(column_y == dy) & (column_d == d) for d in range(channels)] for dy in range(3)]
    z_row = lax.broadcasted_iota(jnp.int32, (nz, depth), 0)
    z_column = lax.rem(lax.broadcasted_iota(jnp.int32, (nz, depth), 1), nz)
    bands = [z_column == lax.rem(z_row + dz - 1 + nz, nz) for dz in range(3)]
    is_low = jnp.broadcast_to(column_kind, (nz, depth)) == 1
    for dx in range(3):
        for c in range(channels):
            values = jnp.zeros((nz, depth), f32)
            for dz in range(3):
                line = jnp.zeros((1, depth), f32)
                for dy in range(3):
                    for d in range(channels):
                        line = jnp.where(
                            picks[dy][d], 0.5 * stencil[c, d, dy * 9 + dz * 3 + dx], line
                        )
                values = values + jnp.where(bands[dz], line, 0.0)
            high = values.astype(bf16).astype(f32)
            low = values - high
            at = (dx * channels + c) * nz
            matrix[at : at + nz, :] = jnp.where(is_low, low, high).astype(bf16)

    for index, (dy, dz) in enumerate(others):
        phase_copy(index).wait_recv()
    own_phase.wait()
    tangent_row = slots[pl.ds(my_load, 1), :][:, TANGENT : TANGENT + 1]
    my_tangent = jnp.broadcast_to(tangent_row, (nz, nx))
    inverse_tangent = 1.0 / my_tangent
    for y in range(ny):
        second = phase_all[y] == 1
        mod = jnp.where(second, my_tangent, 1.0)
        mod_mid[y] = mod
        mod_low[y] = pltpu.roll(mod, nx - 1, 1)
        mod_high[y] = pltpu.roll(mod, 1, 1)
        mod_inv[y] = jnp.where(second, inverse_tangent, 1.0)
    ones = jnp.ones((nz, nx), f32)
    inverse_centre = [1.0 / (ones * stencil[c, c, 13]) for c in range(channels)]

    def put(buffer, y, c, value):
        both = jnp.concatenate([value, value * mod_mid[y]], axis=1)
        high = both.astype(bf16)
        low = (both - high.astype(f32)).astype(bf16)
        places = [y + 1] + ([ny + 1] if y == 0 else []) + ([0] if y == ny - 1 else [])
        for place in places:
            at = place * slot_rows + c * nz
            spread[buffer, at : at + nz, :] = high
            spread[buffer, at + wide : at + wide + nz, :] = high
            spread[buffer, at + 2 * wide : at + 2 * wide + nz, :] = low

    first_weight, weights = chebyshev_weights(SWEEPS)
    quarters = (ngz // CORES, CORES, z_here, nx)
    for y in list(range(y_here, ny)) + list(range(y_here)):
        if y % y_here == 0:
            for index, (dy, dz) in enumerate(others):
                if dy == y // y_here:
                    force_copy(index).wait_recv()
        for c in range(channels):
            value = first_weight * (force[c, y] * inverse_centre[c])
            update[c, y] = value
            field_now[c, y] = value.reshape(quarters)
            put(0, y, c, value)

    pass_on(0)

    def row_product(buffer, y):
        at = y * slot_rows
        return jnp.dot(
            matrix[...], spread[buffer, pl.ds(at, depth), :], preferred_element_type=f32
        )

    def finish_row(product, buffer, y, old_weight, new_weight, last):
        for c in range(channels):
            parts = []
            for dx, mod in enumerate((mod_low, mod_mid, mod_high)):
                row = (dx * channels + c) * nz
                parts.append(
                    mod[y] * product[row : row + nz, :nx] + product[row : row + nz, nx:]
                )
            stiff = parts[1] + pltpu.roll(parts[0], 1, 1) + pltpu.roll(parts[2], nx - 1, 1)
            residual = (force[c, y] - stiff * mod_inv[y]) * inverse_centre[c]
            step = old_weight * update[c, y] + new_weight * residual
            value = field_now[c, y].reshape(nz, nx) + step
            field_now[c, y] = value.reshape(quarters)
            if not last:
                update[c, y] = step
                put(1 - buffer, y, c, value)

    def sweep(k, carry):
        old_weight, new_weight = jnp.float32(weights[0][0]), jnp.float32(weights[0][1])
        for position in range(1, plain):
            old_weight = jnp.where(k == position, weights[position][0], old_weight)
            new_weight = jnp.where(k == position, weights[position][1], new_weight)
        buffer = lax.rem(k, 2)
        product = row_product(buffer, 0)
        for y in range(ny):
            later = row_product(buffer, y + 1) if y + 1 < ny else None
            finish_row(product, buffer, y, old_weight, new_weight, False)
            product = later
        for c, after in enumerate(PASSES):
            if after % ny == 0 and after <= plain * ny:
                pl.when(k == after // ny - 1)(functools.partial(pass_on, c + 1))
        return carry

    plain = len(weights) - SKEWED
    lax.fori_loop(0, plain, sweep, 0)

    sides = [(dy, dz, dz) for dy in range(1, ngy) for dz in range(ngz)]
    sides += [(0, 1, CORES), (0, 2, CORES + turn)]

    groups_here = y_here // SENT_ROWS

    def rows_of(group):
        return pl.ds(group * SENT_ROWS, SENT_ROWS)

    def field_copy(dy, place, dz, group, load):
        to_y, to_z = turned(my_y, dy, ngy), turned(my_z, dz, ngz)
        return pltpu.make_async_remote_copy(
            src_ref=field_now.at[
                :, rows_of(dy * groups_here + group), to_z // CORES, lax.rem(to_z, CORES)
            ],
            dst_ref=fields.at[0, load, :, rows_of(group)],
            send_sem=field_send.at[dy, place, group], recv_sem=field_recv.at[dy, place, group],
            device_id={"gy": to_y, "gz": to_z}, device_id_type=MESH,
        )

    def twin_copy(group):
        return pltpu.make_async_remote_copy(
            src_ref=field_now.at[:, rows_of(group), :, 1 - my_core],
            dst_ref=twin_field.at[:, rows_of(group)],
            send_sem=twin_send.at[group], recv_sem=twin_recv.at[group],
            device_id=mate_id(0, turn), device_id_type=MESH,
        )

    def own_field(group):
        return pltpu.make_async_copy(
            field_now.at[:, rows_of(group), my_z // CORES, my_core],
            fields.at[0, my_load, :, rows_of(group)],
            own_sem.at[2 + group],
        )

    order = skewed_order(ny, y_here, SKEWED)
    product = row_product(plain % 2, order[0][1])
    for place, (level, row) in enumerate(order):
        later = None
        if place + 1 < len(order):
            later = row_product((plain + order[place + 1][0]) % 2, order[place + 1][1])
        last = level == SKEWED - 1
        finish_row(product, (plain + level) % 2, row, *weights[plain + level], last)
        product = later
        group = row // SENT_ROWS
        waiting = [step for step in order[place + 1 :] if step in [
            (SKEWED - 1, group * SENT_ROWS + other) for other in range(SENT_ROWS)
        ]]
        if last and not waiting:
            twin_copy(group).start()
            for side, where, dz in sides:
                if side == group // groups_here:
                    field_copy(side, where, dz, group % groups_here, my_load).start()
            if group < groups_here:
                own_field(group).start()
        for c, after in enumerate(PASSES):
            if after == plain * ny + place + 1 and after > plain * ny:
                pass_on(c + 1)

    for c in range(channels):
        polar_arrival(1 - my_core, c).wait_recv()
        polar_arrival(2, c).wait_recv()
    twin_load = my_load + turn
    slopes = [slot_value(my_load, TANGENT), slot_value(twin_load, TANGENT)]
    totals_of = [[jnp.zeros((z_here, nx), f32) for _ in range(strains)] for _ in range(2)]
    counted = jnp.zeros((z_here, nx), f32)
    corners = [(0, 0)] + twins
    arrived = []
    for _, row in order[-ny:]:
        if row // SENT_ROWS not in arrived:
            arrived.append(row // SENT_ROWS)
    for which in range(2):
        for group in arrived:
            if which:
                twin_copy(group).wait_recv()
            for index, (dy, dz) in enumerate(corners):
                if dy != group // groups_here:
                    continue
                part = lax.rem(my_z // CORES + dz // CORES, ngz // CORES)
                for row in range(group * SENT_ROWS, (group + 1) * SENT_ROWS):
                    y = row % y_here
                    z_at = pl.ds(pl.multiple_of((CORES * part + my_core) * z_here, 8), z_here)
                    second = phase_all[row, z_at, :] == 1
                    mod = jnp.where(second, slopes[which], 1.0)
                    if not which:
                        counted = counted + jnp.where(second, 1.0, 0.0)
                    for c in range(channels):
                        if which:
                            value = twin_field[c, row, part]
                            if index == 0:
                                fields[0, twin_load, c, y] = value
                        else:
                            value = field_now[c, row, part, my_core]
                        flux = mod * value
                        for j in range(strains):
                            weight = polar[c, j, y] if index == 0 else polar_far[index - 1, c, j, y]
                            totals_of[which][j] = totals_of[which][j] + weight * flux

    def whole_sum(values):
        return jnp.sum(jnp.sum(values, axis=0, keepdims=True), axis=1, keepdims=True)

    second_count = whole_sum(counted)
    for which, load in enumerate((my_load, twin_load)):
        line = slots[pl.ds(load, 1), :]
        mod_sum = second_count * line[:, TANGENT : TANGENT + 1] + (
            float(len(twins) + 1) * y_here * z_here * nx - second_count
        )
        line = line * mod_sum
        for j in range(strains):
            line = line + jnp.where(lane_ids[:1] == j, whole_sum(totals_of[which][j]), 0.0)
        stress[lax.rem(load, CAP)] = line * (1.0 / (ny * nz * nx))

    my_macro = my_load // CAP

    def total_copy(dy, dz):
        return pltpu.make_async_remote_copy(
            src_ref=stress, dst_ref=totals.at[my_r, my_core],
            send_sem=total_send.at[dy, dz], recv_sem=total_recv.at[my_r, my_core],
            device_id={"rve": my_macro, **mate_id(dy, dz)}, device_id_type=MESH,
        )

    def total_arrival(group, core):
        return pltpu.make_async_remote_copy(
            src_ref=stress, dst_ref=totals.at[group, core],
            send_sem=total_send.at[0, 0], recv_sem=total_recv.at[group, core],
            device_id={"rve": turned(my_r, 1, groups)}, device_id_type=MESH,
        )

    for dy, dz in others:
        total_copy(dy, dz).start()

    @pl.when(my_macro != my_r)
    def _():
        total_copy(0, 0).start()

    @pl.when(my_macro == my_r)
    def _():
        totals[my_r, my_core] = stress[...]

    for group in range(groups):
        for core in range(CORES):
            @pl.when((my_r != group) | (my_macro != group) | (my_core != core))
            def _():
                total_arrival(group, core).wait_recv()

    mine = tables[my_r]
    answer = jnp.zeros((8, 128), f32)
    for group in range(groups):
        for rank in range(CAP):
            chosen = (mine[:, TARGET : TARGET + 1] == float(group)) & (
                mine[:, RANK : RANK + 1] == float(rank)
            )
            line = totals[group, 0, rank]
            for core in range(1, CORES):
                line = line + totals[group, core, rank]
            answer = answer + jnp.where(chosen, line, 0.0)
    rows_out[...] = answer[:listed, :strains]

    @pl.when(my_macro != my_r)
    def _():
        total_copy(0, 0).wait_send()

    for c in range(channels):
        for index in range(2):
            polar_copy(index, c).wait_send()
        onward_copy(c).wait_send()
    for group in range(groups_here):
        own_field(group).wait()
    for step in range(1, groups):
        table_copy(step, my_r).wait_send()
    for index, (dy, dz) in enumerate(others):
        phase_copy(index).wait_send()
        force_copy(index).wait_send()
        total_copy(dy, dz).wait_send()
    for dy, where, dz in sides:
        load = turned(my_y, -dy, ngy) * ngz + turned(my_z, -dz, ngz)
        for group in range(groups_here):
            field_copy(dy, where, dz, group, my_load).wait_send()
            field_copy(dy, where, dz, group, load).wait_recv()
    for group in range(ngy * groups_here):
        twin_copy(group).wait_send()


def deliver(held_fields, held_rows, fields, rows_out, sem):
    copies = [
        pltpu.make_async_copy(held_fields, fields, sem.at[0]),
        pltpu.make_async_copy(held_rows, rows_out, sem.at[1]),
    ]
    for copy in copies:
        copy.start()
    for copy in copies:
        copy.wait()


def fused_body(strain, tangent, yield_list, destination, phase_map, polarization, stencil):
    groups, ngy, ngz = (lax.axis_size(name) for name in ("rve", "gy", "gz"))
    channels = polarization.shape[1]
    strains = polarization.shape[2]
    y_here, z_here, nx = polarization.shape[3:]
    ny, nz = y_here * ngy, z_here * ngz
    loads = groups * CAP
    count = ngy * ngz
    f32 = jnp.float32
    slot_rows = 3 * channels * nz
    vmem = pl.BlockSpec(memory_space=pltpu.VMEM)
    hbm = pl.BlockSpec(memory_space=pltpu.HBM)
    cell = pltpu.VMEM((ny, nz, nx), f32)
    vector = pltpu.VMEM((channels, ny, nz, nx), f32)

    def dma(*shape):
        return pltpu.SemaphoreType.DMA(shape)

    held_fields, held_rows = pl.pallas_call(
        functools.partial(kernel, groups, ngy, ngz),
        out_shape=(
            jax.ShapeDtypeStruct((1, loads, channels, y_here, z_here, nx), f32),
            jax.ShapeDtypeStruct((yield_list.shape[0], strains), f32),
        ),
        in_specs=[hbm] * 7,
        out_specs=(vmem, vmem),
        scratch_shapes=[
            pltpu.SMEM(strain.shape, f32),
            pltpu.SMEM(tangent.shape, f32),
            pltpu.SMEM(yield_list.shape, jnp.int32),
            pltpu.SMEM(yield_list.shape, jnp.int32),
            pltpu.SMEM(stencil.shape, f32),
            pltpu.VMEM(polarization.shape[1:], f32),
            dma(6),
            pltpu.VMEM((groups, 8, 128), f32),
            pltpu.VMEM((loads, 128), f32),
            pltpu.VMEM((ny, nz, nx), jnp.int32),
            pltpu.VMEM((3, *polarization.shape[1:]), f32),
            pltpu.VMEM((channels, ny, ngz // CORES, z_here, nx), f32),
            pltpu.VMEM((count, channels, y_here, z_here, nx), f32),
            vector,
            pltpu.VMEM((3 * channels * nz, 3 * slot_rows), jnp.bfloat16),
            pltpu.VMEM((2, (ny + 2) * slot_rows, 2 * nx), jnp.bfloat16),
            pltpu.VMEM((channels, ny, ngz // CORES, CORES, z_here, nx), f32),
            vector,
            cell, cell, cell, cell,
            pltpu.VMEM((CAP, 1, 128), f32),
            pltpu.VMEM((groups, CORES, CAP, 1, 128), f32),
            dma(groups), dma(groups), dma(count), dma(count),
            dma(3, channels), dma(3, channels),
            dma(ny), dma(ny),
            dma(count), dma(count),
            dma(ngy, ngz, y_here), dma(ngy, ngz, y_here),
            dma(ngy, ngz), dma(groups, CORES), dma(2 + y_here),
        ],
        compiler_params=pltpu.CompilerParams(
            collective_id=0, has_side_effects=True, vmem_limit_bytes=40 * 1024 * 1024
        ),
    )(*[
        pltpu.with_memory_space_constraint(argument, pltpu.HBM)
        for argument in (
            strain, tangent, yield_list, destination[:, 0], stencil, phase_map, polarization
        )
    ])
    return pl.pallas_call(
        deliver,
        out_shape=(
            jax.ShapeDtypeStruct(held_fields.shape, f32),
            jax.ShapeDtypeStruct(held_rows.shape, f32),
        ),
        in_specs=[vmem, vmem],
        out_specs=(hbm, hbm),
        scratch_shapes=[dma(2)],
        compiler_params=pltpu.CompilerParams(vmem_limit_bytes=4 * 1024 * 1024),
    )(held_fields, held_rows)


def body_for(mesh):
    def chosen(*arguments):
        strain, _, yield_list, _, phase_map, _, _ = arguments
        loads = lax.axis_size("rve") * CAP
        one_load_each = lax.axis_size("gy") == 2 and lax.axis_size("gz") == 2 * CORES
        tiled = phase_map.shape[2] == 8 and phase_map.shape[3] == 128 and loads == 8
        if one_load_each and tiled and yield_list.shape[0] <= 8:
            return fused_body(*arguments)
        return body(*arguments)

    return chosen


def solution(mesh):
    return jax.shard_map(
        body_for(mesh),
        mesh=mesh,
        in_specs=(
            P("rve", None),
            P("rve"),
            P("rve"),
            P("rve", None),
            P("rve", "gy", "gz", None),
            P("rve", None, None, "gy", "gz", None),
            P(),
        ),
        out_specs=(P("rve", None, None, "gy", "gz", None), P("rve", None)),
        check_vma=False,
    )
```

```python
import functools

import jax
import jax.numpy as jnp
from jax import lax
from jax.experimental import pallas as pl
from jax.experimental.pallas import tpu as pltpu
from jax.sharding import PartitionSpec as P

CAP = 2
CORES = 2
SKEWED = 1
PASSES = (16,)
STRAIGHT = (2,)
SENT_ROWS = 2
SWEEPS = 6
MESH = pl.DeviceIdType.MESH
TANGENT, TARGET, RANK, LISTED = 6, 7, 8, 9


FULL_PRECISION = lax.Precision.HIGHEST
LOWER_BOUND = 0.05
UPPER_BOUND = 1.95


def padded(block, sides, width):
    for axis, dim in sides:
        count = lax.axis_size(axis)
        forward = [(i, i + 1) for i in range(count - 1)]
        forward.append((count - 1, 0))
        backward = [(target, source) for source, target in forward]
        low = lax.ppermute(
            lax.slice_in_dim(block, block.shape[dim] - width, None, axis=dim), axis, forward
        )
        high = lax.ppermute(lax.slice_in_dim(block, 0, width, axis=dim), axis, backward)
        block = jnp.concatenate([low, block, high], axis=dim)
    return block


def chebyshev_weights(sweep_count):
    centre_value = 0.5 * (UPPER_BOUND + LOWER_BOUND)
    half_width = 0.5 * (UPPER_BOUND - LOWER_BOUND)
    ratio_value = centre_value / half_width
    rho_before = 1.0 / ratio_value
    weights = []
    for sweep_index in range(1, sweep_count):
        rho_after = 1.0 / (2.0 * ratio_value - rho_before)
        weights.append((rho_after * rho_before, 2.0 * rho_after / half_width))
        rho_before = rho_after
    return (1.0 / centre_value, weights)


def skewed_order(rows, half, levels):
    def needed(level, row):
        steps = [(level, row)]
        if level:
            for shift in (-1, 0, 1):
                steps += needed(level - 1, (row + shift) % rows)
        return steps

    finals = []
    for away in range(rows // 2):
        finals += [(half + away) % rows, (half - 1 - away) % rows]
    finals = [row for pair in range(0, rows, 4) for row in finals[pair : pair + 4 : 2] + finals[pair + 1 : pair + 4 : 2]]
    placed = {}
    order = []
    while len(order) < rows * levels:
        choice = None
        for lag in (2, 1):
            for final in finals:
                for level, row in sorted(set(needed(levels - 1, final))):
                    inputs = needed(level, row)[1:]
                    ready = all(placed.get(step, rows * levels) <= len(order) - lag for step in inputs)
                    if choice is None and (level, row) not in placed and ready:
                        choice = (level, row)
        placed[choice] = len(order)
        order.append(choice)
    return order


def trim_margin(values_in, margin_have, margin_want, first_dim):
    excess = margin_have - margin_want
    values_in = lax.slice_in_dim(
        values_in, excess, values_in.shape[first_dim] - excess, axis=first_dim
    )
    return lax.slice_in_dim(
        values_in, excess, values_in.shape[first_dim + 1] - excess, axis=first_dim + 1
    )


def apply_stiffness(field_now, moduli, stencil):
    inner_y = field_now.shape[2] - 2
    inner_z = field_now.shape[3] - 2
    centre_mod = moduli[:, 1 : 1 + inner_y, 1 : 1 + inner_z, :]
    running = [None, None, None]
    for shift_y in (-1, 0, 1):
        for shift_z in (-1, 0, 1):
            shifted = field_now[
                :, :, 1 + shift_y : 1 + shift_y + inner_y, 1 + shift_z : 1 + shift_z + inner_z, :
            ]
            shifted_mod = moduli[
                :, 1 + shift_y : 1 + shift_y + inner_y, 1 + shift_z : 1 + shift_z + inner_z, :
            ]
            for shift_x in (-1, 0, 1):
                if shift_x != 0:
                    rolled = jnp.roll(shifted, -shift_x, axis=4)
                    rolled_mod = jnp.roll(shifted_mod, -shift_x, axis=3)
                else:
                    rolled = shifted
                    rolled_mod = shifted_mod
                offset_index = (shift_y + 1) * 9 + (shift_z + 1) * 3 + (shift_x + 1)
                edge_mod = 0.5 * (centre_mod + rolled_mod)
                weighted = [edge_mod * rolled[:, channel_in] for channel_in in range(3)]
                for channel_out in range(3):
                    mixed = stencil[channel_out, 0, offset_index] * weighted[0]
                    mixed = mixed + stencil[channel_out, 1, offset_index] * weighted[1]
                    mixed = mixed + stencil[channel_out, 2, offset_index] * weighted[2]
                    if running[channel_out] is None:
                        running[channel_out] = mixed
                    else:
                        running[channel_out] = running[channel_out] + mixed
    return jnp.stack(running, axis=1)


def body(strain, tangent, yield_list, destination, phase_map, polarization, stencil):
    groups = lax.axis_size("rve")
    rows_here = strain.shape[0]
    yield_count = yield_list.shape[0]
    picker = (jnp.arange(rows_here, dtype=jnp.int32)[None, :] == yield_list[:, None]).astype(
        jnp.float32
    )
    row_strain = jnp.dot(picker, strain, precision=FULL_PRECISION)
    row_tangent = jnp.dot(picker, tangent, precision=FULL_PRECISION)
    target = destination[:, 0]
    positions = jnp.arange(yield_count, dtype=jnp.int32)
    earlier = (target[:, None] == target[None, :]) & (positions[None, :] < positions[:, None])
    rank_in = jnp.sum(earlier.astype(jnp.int32), axis=1)
    group_ids = jnp.arange(groups, dtype=jnp.int32)
    slot_ids = jnp.arange(CAP, dtype=jnp.int32)
    onehot = (
        (target[None, None, :] == group_ids[:, None, None])
        & (rank_in[None, None, :] == slot_ids[None, :, None])
    ).astype(jnp.float32)
    packet = jnp.einsum("gci,ij->gcj", onehot, row_strain, precision=FULL_PRECISION)
    packet_tangent = (
        jnp.einsum("gci,i->gc", onehot, row_tangent, precision=FULL_PRECISION)
        + 1.0
        - jnp.sum(onehot, axis=2)
    )
    parcel = jnp.concatenate([packet, packet_tangent[:, :, None]], axis=2)
    arrived = lax.all_to_all(parcel, "rve", split_axis=0, concat_axis=0, tiled=True)
    slot_strain = arrived[:, :, :6].reshape(groups * CAP, 6)
    slot_tangent = arrived[:, :, 6].reshape(groups * CAP)
    phase_wide = padded(phase_map[0], (("gy", 0), ("gz", 1)), 2)
    moduli_wide = jnp.where(
        phase_wide[None] == 1, slot_tangent[:, None, None, None], jnp.float32(1.0)
    )
    moduli_core = trim_margin(moduli_wide, 2, 0, 1)
    moduli_one = trim_margin(moduli_wide, 2, 1, 1)
    polar_local = polarization[0]
    centre_diag = jnp.diagonal(stencil[:, :, 13])
    body_force = moduli_core[:, None] * jnp.einsum(
        "cjyzx,lj->lcyzx", polar_local, slot_strain, precision=FULL_PRECISION
    )
    inverse_diag = 1.0 / (centre_diag[None, :, None, None, None] * moduli_core[:, None])
    first_weight, weights = chebyshev_weights(SWEEPS)
    update = first_weight * (body_force * inverse_diag)
    field_now = update
    for old_weight, new_weight in weights:
        wrapped = padded(field_now, (("gy", 2), ("gz", 3)), 1)
        residual_now = body_force - apply_stiffness(wrapped, moduli_one, stencil)
        update = old_weight * update + new_weight * (residual_now * inverse_diag)
        field_now = field_now + update
    coupled = jnp.einsum(
        "cjyzx,lcyzx->lj", polar_local, moduli_core[:, None] * field_now, precision=FULL_PRECISION
    )
    partial_value = coupled + slot_strain * jnp.sum(moduli_core, axis=(1, 2, 3))[:, None]
    total_cells = (
        lax.axis_size("gy")
        * lax.axis_size("gz")
        * field_now.shape[2]
        * field_now.shape[3]
        * field_now.shape[4]
    )
    summed = lax.psum(partial_value, ("gy", "gz")) / total_cells
    returned = lax.all_to_all(
        summed.reshape(groups, CAP, 6), "rve", split_axis=0, concat_axis=0, tiled=True
    )
    stress_rows = jnp.einsum("gci,gcj->ij", onehot, returned, precision=FULL_PRECISION)
    return (field_now[None], stress_rows)


def kernel(
    groups, ngy, ngz,
    strain_hbm, tangent_hbm, yield_hbm, destination_hbm, stencil_hbm, phase_hbm, polar_hbm,
    fields, rows_out,
    strain, tangent, yield_list, destination, stencil, polar, load_sem,
    tables, slots, phase_all, polar_far, twin_field, force_out, force, matrix, spread, field_now, update,
    mod_mid, mod_low, mod_high, mod_inv, stress, totals,
    table_send, table_recv, phase_send, phase_recv, polar_send, polar_recv,
    twin_send, twin_recv, force_send, force_recv,
    field_send, field_recv, total_send, total_recv, own_sem,
):
    f32, bf16 = jnp.float32, jnp.bfloat16
    channels, strains = polar.shape[:2]
    y_here, z_here, nx = polar.shape[2:]
    ny, nz = y_here * ngy, z_here * ngz
    loaded = [
        pltpu.make_async_copy(source, held, load_sem.at[index])
        for index, (source, held) in enumerate(
            [
                (destination_hbm, destination), (yield_hbm, yield_list), (strain_hbm, strain),
                (tangent_hbm, tangent), (polar_hbm.at[0], polar), (stencil_hbm, stencil),
            ]
        )
    ]
    wide = channels * nz
    slot_rows = 3 * wide
    depth = 3 * slot_rows
    listed = yield_list.shape[0]
    loads = groups * CAP
    my_r, my_y, my_z = lax.axis_index("rve"), lax.axis_index("gy"), lax.axis_index("gz")
    my_load = my_y * ngz + my_z

    def turned(base, step, count):
        return lax.rem(base + step + count, count)

    mates = [(dy, dz) for dy in list(range(1, ngy)) + [0] for dz in list(range(1, ngz)) + [0]]
    others = [mate for mate in mates if mate != (0, 0)]

    def mate_id(dy, dz):
        return {"gy": turned(my_y, dy, ngy), "gz": turned(my_z, dz, ngz)}

    def block(dy):
        y_at = -dy % ngy * y_here
        z_at = pl.multiple_of(my_z * z_here, 8)
        return pl.ds(y_at, y_here), pl.ds(z_at, z_here)

    barrier = pltpu.get_barrier_semaphore()
    for step in range(1, groups):
        pl.semaphore_signal(
            barrier, inc=1, device_id={"rve": turned(my_r, step, groups)}, device_id_type=MESH
        )
    for copy in loaded[:4]:
        copy.start()
    for dy, dz in others:
        pl.semaphore_signal(barrier, inc=1, device_id=mate_id(dy, dz), device_id_type=MESH)
    for copy in loaded[4:]:
        copy.start()
    for copy in loaded[:4]:
        copy.wait()
    row_ids = lax.broadcasted_iota(jnp.int32, (8, 128), 0)
    lane_ids = lax.broadcasted_iota(jnp.int32, (8, 128), 1)
    table = jnp.zeros((8, 128), f32)
    for i in range(listed):
        point, target = yield_list[i], destination[i]
        rank = jnp.int32(0)
        for k in range(i):
            rank = rank + jnp.where(destination[k] == target, 1, 0)
        values = [strain[point, j] for j in range(strains)]
        values += [tangent[point], target.astype(f32), rank.astype(f32), jnp.float32(1.0)]
        for j, value in enumerate(values):
            table = jnp.where((row_ids == i) & (lane_ids == j), value, table)
    tables[my_r] = table

    pl.semaphore_wait(barrier, len(others) + groups - 1)

    def table_copy(step, owner):
        return pltpu.make_async_remote_copy(
            src_ref=tables.at[my_r], dst_ref=tables.at[owner],
            send_sem=table_send.at[step], recv_sem=table_recv.at[step],
            device_id={"rve": turned(my_r, step, groups)}, device_id_type=MESH,
        )

    def phase_copy(index):
        to_y, to_z = others[index]
        y_at, z_at = block(to_y)
        return pltpu.make_async_remote_copy(
            src_ref=phase_hbm.at[0], dst_ref=phase_all.at[y_at, z_at],
            send_sem=phase_send.at[index], recv_sem=phase_recv.at[index],
            device_id=mate_id(to_y, to_z), device_id_type=MESH,
        )

    across, along, corner = (1, 0), (0, CORES), (1, CORES)
    twins = [across, along, corner]
    my_core = lax.rem(my_z, CORES)
    turn = 1 - 2 * my_core

    def polar_copy(index, c):
        return pltpu.make_async_remote_copy(
            src_ref=polar_hbm.at[0, c], dst_ref=polar_far.at[index, c],
            send_sem=polar_send.at[index, c], recv_sem=polar_recv.at[index, c],
            device_id=mate_id(*twins[index]), device_id_type=MESH,
        )

    def polar_arrival(index, c):
        return pltpu.make_async_remote_copy(
            src_ref=polar_hbm.at[0, c], dst_ref=polar_far.at[index, c],
            send_sem=polar_send.at[index, c], recv_sem=polar_recv.at[index, c],
            device_id=mate_id(0, turn), device_id_type=MESH,
        )

    def onward_copy(c):
        return pltpu.make_async_remote_copy(
            src_ref=polar_far.at[my_core, c], dst_ref=polar_far.at[2, c],
            send_sem=polar_send.at[2, c], recv_sem=polar_recv.at[2, c],
            device_id=mate_id(my_core, CORES * (1 - my_core)), device_id_type=MESH,
        )

    def send_polar(channels_now):
        for c in channels_now:
            for index in range(3 if c in STRAIGHT else 2):
                polar_copy(index, c).start()

    def pass_on(c):
        polar_arrival(my_core, c).wait_recv()
        onward_copy(c).start()

    for step in range(1, groups):
        table_copy(step, my_r).start()
    for index in range(len(others)):
        phase_copy(index).start()
    own_y, own_z = block(0)
    own_phase = pltpu.make_async_copy(phase_hbm.at[0], phase_all.at[own_y, own_z], own_sem.at[0])
    own_phase.start()
    send_polar(range(1))

    for step in range(1, groups):
        table_copy(step, turned(my_r, -step, groups)).wait_recv()
    for source in range(groups):
        heard = tables[source]
        named = (heard[:, TARGET : TARGET + 1] == my_r.astype(f32)) & (
            heard[:, LISTED : LISTED + 1] == 1.0
        )
        for rank in range(CAP):
            chosen = named & (heard[:, RANK : RANK + 1] == float(rank))
            line = jnp.sum(jnp.where(chosen, heard, 0.0), axis=0, keepdims=True)
            missing = 1.0 - line[:, LISTED : LISTED + 1]
            line = line + jnp.where(lane_ids[:1] == TANGENT, missing, 0.0)
            at = source * CAP + rank
            slots[at : at + 1, :] = line

    loaded[4].wait()

    def slot_value(load, index):
        return jnp.broadcast_to(slots[pl.ds(load, 1), :][:, index : index + 1], (8, 128))

    def force_copy(index):
        y_at, z_at = block(others[index][0])
        return pltpu.make_async_remote_copy(
            src_ref=force_out.at[index], dst_ref=force.at[:, y_at, z_at],
            send_sem=force_send.at[index], recv_sem=force_recv.at[index],
            device_id=mate_id(*others[index]), device_id_type=MESH,
        )

    for index, (dy, dz) in enumerate(mates):
        load = turned(my_y, dy, ngy) * ngz + turned(my_z, dz, ngz)
        strain_of = [slot_value(load, j) for j in range(strains)]
        for c in range(channels):
            for y in range(y_here):
                value = polar[c, 0, y] * strain_of[0]
                for j in range(1, strains):
                    value = value + polar[c, j, y] * strain_of[j]
                if (dy, dz) == (0, 0):
                    force[c, y, own_z, :] = value
                else:
                    force_out[index, c, y] = value
        if (dy, dz) != (0, 0):
            force_copy(index).start()

    send_polar(range(1, channels))
    loaded[5].wait()
    column = lax.broadcasted_iota(jnp.int32, (1, depth), 1)
    column_y = column // slot_rows
    column_kind = lax.rem(column, slot_rows) // wide
    column_d = lax.rem(column, wide) // nz
    picks = [[(column_y == dy) & (column_d == d) for d in range(channels)] for dy in range(3)]
    z_row = lax.broadcasted_iota(jnp.int32, (nz, depth), 0)
    z_column = lax.rem(lax.broadcasted_iota(jnp.int32, (nz, depth), 1), nz)
    bands = [z_column == lax.rem(z_row + dz - 1 + nz, nz) for dz in range(3)]
    is_low = jnp.broadcast_to(column_kind, (nz, depth)) == 1
    for dx in range(3):
        for c in range(channels):
            values = jnp.zeros((nz, depth), f32)
            for dz in range(3):
                line = jnp.zeros((1, depth), f32)
                for dy in range(3):
                    for d in range(channels):
                        line = jnp.where(
                            picks[dy][d], 0.5 * stencil[c, d, dy * 9 + dz * 3 + dx], line
                        )
                values = values + jnp.where(bands[dz], line, 0.0)
            high = values.astype(bf16).astype(f32)
            low = values - high
            at = (dx * channels + c) * nz
            matrix[at : at + nz, :] = jnp.where(is_low, low, high).astype(bf16)

    for index, (dy, dz) in enumerate(others):
        phase_copy(index).wait_recv()
    own_phase.wait()
    tangent_row = slots[pl.ds(my_load, 1), :][:, TANGENT : TANGENT + 1]
    my_tangent = jnp.broadcast_to(tangent_row, (nz, nx))
    inverse_tangent = 1.0 / my_tangent
    for y in range(ny):
        second = phase_all[y] == 1
        mod = jnp.where(second, my_tangent, 1.0)
        mod_mid[y] = mod
        mod_low[y] = pltpu.roll(mod, nx - 1, 1)
        mod_high[y] = pltpu.roll(mod, 1, 1)
        mod_inv[y] = jnp.where(second, inverse_tangent, 1.0)
    ones = jnp.ones((nz, nx), f32)
    inverse_centre = [1.0 / (ones * stencil[c, c, 13]) for c in range(channels)]

    def put(buffer, y, c, value):
        both = jnp.concatenate([value, value * mod_mid[y]], axis=1)
        high = both.astype(bf16)
        low = (both - high.astype(f32)).astype(bf16)
        places = [y + 1] + ([ny + 1] if y == 0 else []) + ([0] if y == ny - 1 else [])
        for place in places:
            at = place * slot_rows + c * nz
            spread[buffer, at : at + nz, :] = high
            spread[buffer, at + wide : at + wide + nz, :] = high
            spread[buffer, at + 2 * wide : at + 2 * wide + nz, :] = low

    first_weight, weights = chebyshev_weights(SWEEPS)
    quarters = (ngz // CORES, CORES, z_here, nx)
    for y in list(range(y_here, ny)) + list(range(y_here)):
        if y % y_here == 0:
            for index, (dy, dz) in enumerate(others):
                if dy == y // y_here:
                    force_copy(index).wait_recv()
        for c in range(channels):
            value = first_weight * (force[c, y] * inverse_centre[c])
            update[c, y] = value
            field_now[c, y] = value.reshape(quarters)
            put(0, y, c, value)

    pass_on(0)

    def row_product(buffer, y):
        at = y * slot_rows
        return jnp.dot(
            matrix[...], spread[buffer, pl.ds(at, depth), :], preferred_element_type=f32
        )

    def finish_row(product, buffer, y, old_weight, new_weight, last):
        for c in range(channels):
            parts = []
            for dx, mod in enumerate((mod_low, mod_mid, mod_high)):
                row = (dx * channels + c) * nz
                parts.append(
                    mod[y] * product[row : row + nz, :nx] + product[row : row + nz, nx:]
                )
            stiff = parts[1] + pltpu.roll(parts[0], 1, 1) + pltpu.roll(parts[2], nx - 1, 1)
            residual = (force[c, y] - stiff * mod_inv[y]) * inverse_centre[c]
            step = old_weight * update[c, y] + new_weight * residual
            value = field_now[c, y].reshape(nz, nx) + step
            field_now[c, y] = value.reshape(quarters)
            if not last:
                update[c, y] = step
                put(1 - buffer, y, c, value)

    def sweep(k, carry):
        old_weight, new_weight = jnp.float32(weights[0][0]), jnp.float32(weights[0][1])
        for position in range(1, plain):
            old_weight = jnp.where(k == position, weights[position][0], old_weight)
            new_weight = jnp.where(k == position, weights[position][1], new_weight)
        buffer = lax.rem(k, 2)
        product = row_product(buffer, 0)
        for y in range(ny):
            later = row_product(buffer, y + 1) if y + 1 < ny else None
            finish_row(product, buffer, y, old_weight, new_weight, False)
            product = later
        for c, after in enumerate(PASSES):
            if after % ny == 0 and after <= plain * ny:
                pl.when(k == after // ny - 1)(functools.partial(pass_on, c + 1))
        return carry

    plain = len(weights) - SKEWED
    lax.fori_loop(0, plain, sweep, 0)

    sides = [(dy, dz, dz) for dy in range(1, ngy) for dz in range(ngz)]
    sides += [(0, 1, CORES), (0, 2, CORES + turn)]

    groups_here = y_here // SENT_ROWS

    def rows_of(group):
        return pl.ds(group * SENT_ROWS, SENT_ROWS)

    def field_copy(dy, place, dz, group, load):
        to_y, to_z = turned(my_y, dy, ngy), turned(my_z, dz, ngz)
        return pltpu.make_async_remote_copy(
            src_ref=field_now.at[
                :, rows_of(dy * groups_here + group), to_z // CORES, lax.rem(to_z, CORES)
            ],
            dst_ref=fields.at[0, load, :, rows_of(group)],
            send_sem=field_send.at[dy, place, group], recv_sem=field_recv.at[dy, place, group],
            device_id={"gy": to_y, "gz": to_z}, device_id_type=MESH,
        )

    def twin_copy(group):
        return pltpu.make_async_remote_copy(
            src_ref=field_now.at[:, rows_of(group), :, 1 - my_core],
            dst_ref=twin_field.at[:, rows_of(group)],
            send_sem=twin_send.at[group], recv_sem=twin_recv.at[group],
            device_id=mate_id(0, turn), device_id_type=MESH,
        )

    def own_field(group):
        return pltpu.make_async_copy(
            field_now.at[:, rows_of(group), my_z // CORES, my_core],
            fields.at[0, my_load, :, rows_of(group)],
            own_sem.at[2 + group],
        )

    order = skewed_order(ny, y_here, SKEWED)
    product = row_product(plain % 2, order[0][1])
    for place, (level, row) in enumerate(order):
        later = None
        if place + 1 < len(order):
            later = row_product((plain + order[place + 1][0]) % 2, order[place + 1][1])
        last = level == SKEWED - 1
        finish_row(product, (plain + level) % 2, row, *weights[plain + level], last)
        product = later
        group = row // SENT_ROWS
        waiting = [step for step in order[place + 1 :] if step in [
            (SKEWED - 1, group * SENT_ROWS + other) for other in range(SENT_ROWS)
        ]]
        if last and not waiting:
            twin_copy(group).start()
            for side, where, dz in sides:
                if side == group // groups_here:
                    field_copy(side, where, dz, group % groups_here, my_load).start()
            if group < groups_here:
                own_field(group).start()
        for c, after in enumerate(PASSES):
            if after == plain * ny + place + 1 and after > plain * ny:
                pass_on(c + 1)

    for c in range(channels):
        polar_arrival(1 - my_core, c).wait_recv()
        if c in STRAIGHT:
            polar_arrival(my_core, c).wait_recv()
        polar_arrival(2, c).wait_recv()
    twin_load = my_load + turn
    slopes = [slot_value(my_load, TANGENT), slot_value(twin_load, TANGENT)]
    totals_of = [[jnp.zeros((z_here, nx), f32) for _ in range(strains)] for _ in range(2)]
    counted = jnp.zeros((z_here, nx), f32)
    corners = [(0, 0)] + twins
    arrived = []
    for _, row in order[-ny:]:
        if row // SENT_ROWS not in arrived:
            arrived.append(row // SENT_ROWS)
    for which in range(2):
        for group in arrived:
            if which:
                twin_copy(group).wait_recv()
            for index, (dy, dz) in enumerate(corners):
                if dy != group // groups_here:
                    continue
                part = lax.rem(my_z // CORES + dz // CORES, ngz // CORES)
                for row in range(group * SENT_ROWS, (group + 1) * SENT_ROWS):
                    y = row % y_here
                    z_at = pl.ds(pl.multiple_of((CORES * part + my_core) * z_here, 8), z_here)
                    second = phase_all[row, z_at, :] == 1
                    mod = jnp.where(second, slopes[which], 1.0)
                    if not which:
                        counted = counted + jnp.where(second, 1.0, 0.0)
                    for c in range(channels):
                        if which:
                            value = twin_field[c, row, part]
                            if index == 0:
                                fields[0, twin_load, c, y] = value
                        else:
                            value = field_now[c, row, part, my_core]
                        flux = mod * value
                        for j in range(strains):
                            weight = polar[c, j, y] if index == 0 else polar_far[index - 1, c, j, y]
                            totals_of[which][j] = totals_of[which][j] + weight * flux

    def whole_sum(values):
        return jnp.sum(jnp.sum(values, axis=0, keepdims=True), axis=1, keepdims=True)

    second_count = whole_sum(counted)
    for which, load in enumerate((my_load, twin_load)):
        line = slots[pl.ds(load, 1), :]
        mod_sum = second_count * line[:, TANGENT : TANGENT + 1] + (
            float(len(twins) + 1) * y_here * z_here * nx - second_count
        )
        line = line * mod_sum
        for j in range(strains):
            line = line + jnp.where(lane_ids[:1] == j, whole_sum(totals_of[which][j]), 0.0)
        stress[lax.rem(load, CAP)] = line * (1.0 / (ny * nz * nx))

    my_macro = my_load // CAP

    def total_copy(dy, dz):
        return pltpu.make_async_remote_copy(
            src_ref=stress, dst_ref=totals.at[my_r, my_core],
            send_sem=total_send.at[dy, dz], recv_sem=total_recv.at[my_r, my_core],
            device_id={"rve": my_macro, **mate_id(dy, dz)}, device_id_type=MESH,
        )

    def total_arrival(group, core):
        return pltpu.make_async_remote_copy(
            src_ref=stress, dst_ref=totals.at[group, core],
            send_sem=total_send.at[0, 0], recv_sem=total_recv.at[group, core],
            device_id={"rve": turned(my_r, 1, groups)}, device_id_type=MESH,
        )

    for dy, dz in others:
        total_copy(dy, dz).start()

    @pl.when(my_macro != my_r)
    def _():
        total_copy(0, 0).start()

    @pl.when(my_macro == my_r)
    def _():
        totals[my_r, my_core] = stress[...]

    for group in range(groups):
        for core in range(CORES):
            @pl.when((my_r != group) | (my_macro != group) | (my_core != core))
            def _():
                total_arrival(group, core).wait_recv()

    mine = tables[my_r]
    answer = jnp.zeros((8, 128), f32)
    for group in range(groups):
        for rank in range(CAP):
            chosen = (mine[:, TARGET : TARGET + 1] == float(group)) & (
                mine[:, RANK : RANK + 1] == float(rank)
            )
            line = totals[group, 0, rank]
            for core in range(1, CORES):
                line = line + totals[group, core, rank]
            answer = answer + jnp.where(chosen, line, 0.0)
    rows_out[...] = answer[:listed, :strains]

    @pl.when(my_macro != my_r)
    def _():
        total_copy(0, 0).wait_send()

    for c in range(channels):
        for index in range(2):
            polar_copy(index, c).wait_send()
        (polar_copy(2, c) if c in STRAIGHT else onward_copy(c)).wait_send()
    for group in range(groups_here):
        own_field(group).wait()
    for step in range(1, groups):
        table_copy(step, my_r).wait_send()
    for index, (dy, dz) in enumerate(others):
        phase_copy(index).wait_send()
        force_copy(index).wait_send()
        total_copy(dy, dz).wait_send()
    for dy, where, dz in sides:
        load = turned(my_y, -dy, ngy) * ngz + turned(my_z, -dz, ngz)
        for group in range(groups_here):
            field_copy(dy, where, dz, group, my_load).wait_send()
            field_copy(dy, where, dz, group, load).wait_recv()
    for group in range(ngy * groups_here):
        twin_copy(group).wait_send()


def deliver(held_fields, held_rows, fields, rows_out, sem):
    copies = [
        pltpu.make_async_copy(held_fields, fields, sem.at[0]),
        pltpu.make_async_copy(held_rows, rows_out, sem.at[1]),
    ]
    for copy in copies:
        copy.start()
    for copy in copies:
        copy.wait()


def fused_body(strain, tangent, yield_list, destination, phase_map, polarization, stencil):
    groups, ngy, ngz = (lax.axis_size(name) for name in ("rve", "gy", "gz"))
    channels = polarization.shape[1]
    strains = polarization.shape[2]
    y_here, z_here, nx = polarization.shape[3:]
    ny, nz = y_here * ngy, z_here * ngz
    loads = groups * CAP
    count = ngy * ngz
    f32 = jnp.float32
    slot_rows = 3 * channels * nz
    vmem = pl.BlockSpec(memory_space=pltpu.VMEM)
    hbm = pl.BlockSpec(memory_space=pltpu.HBM)
    cell = pltpu.VMEM((ny, nz, nx), f32)
    vector = pltpu.VMEM((channels, ny, nz, nx), f32)

    def dma(*shape):
        return pltpu.SemaphoreType.DMA(shape)

    held_fields, held_rows = pl.pallas_call(
        functools.partial(kernel, groups, ngy, ngz),
        out_shape=(
            jax.ShapeDtypeStruct((1, loads, channels, y_here, z_here, nx), f32),
            jax.ShapeDtypeStruct((yield_list.shape[0], strains), f32),
        ),
        in_specs=[hbm] * 7,
        out_specs=(vmem, vmem),
        scratch_shapes=[
            pltpu.SMEM(strain.shape, f32),
            pltpu.SMEM(tangent.shape, f32),
            pltpu.SMEM(yield_list.shape, jnp.int32),
            pltpu.SMEM(yield_list.shape, jnp.int32),
            pltpu.SMEM(stencil.shape, f32),
            pltpu.VMEM(polarization.shape[1:], f32),
            dma(6),
            pltpu.VMEM((groups, 8, 128), f32),
            pltpu.VMEM((loads, 128), f32),
            pltpu.VMEM((ny, nz, nx), jnp.int32),
            pltpu.VMEM((3, *polarization.shape[1:]), f32),
            pltpu.VMEM((channels, ny, ngz // CORES, z_here, nx), f32),
            pltpu.VMEM((count, channels, y_here, z_here, nx), f32),
            vector,
            pltpu.VMEM((3 * channels * nz, 3 * slot_rows), jnp.bfloat16),
            pltpu.VMEM((2, (ny + 2) * slot_rows, 2 * nx), jnp.bfloat16),
            pltpu.VMEM((channels, ny, ngz // CORES, CORES, z_here, nx), f32),
            vector,
            cell, cell, cell, cell,
            pltpu.VMEM((CAP, 1, 128), f32),
            pltpu.VMEM((groups, CORES, CAP, 1, 128), f32),
            dma(groups), dma(groups), dma(count), dma(count),
            dma(3, channels), dma(3, channels),
            dma(ny), dma(ny),
            dma(count), dma(count),
            dma(ngy, ngz, y_here), dma(ngy, ngz, y_here),
            dma(ngy, ngz), dma(groups, CORES), dma(2 + y_here),
        ],
        compiler_params=pltpu.CompilerParams(
            collective_id=0, has_side_effects=True, vmem_limit_bytes=40 * 1024 * 1024
        ),
    )(*[
        pltpu.with_memory_space_constraint(argument, pltpu.HBM)
        for argument in (
            strain, tangent, yield_list, destination[:, 0], stencil, phase_map, polarization
        )
    ])
    return pl.pallas_call(
        deliver,
        out_shape=(
            jax.ShapeDtypeStruct(held_fields.shape, f32),
            jax.ShapeDtypeStruct(held_rows.shape, f32),
        ),
        in_specs=[vmem, vmem],
        out_specs=(hbm, hbm),
        scratch_shapes=[dma(2)],
        compiler_params=pltpu.CompilerParams(vmem_limit_bytes=4 * 1024 * 1024),
    )(held_fields, held_rows)


def body_for(mesh):
    def chosen(*arguments):
        strain, _, yield_list, _, phase_map, _, _ = arguments
        loads = lax.axis_size("rve") * CAP
        one_load_each = lax.axis_size("gy") == 2 and lax.axis_size("gz") == 2 * CORES
        tiled = phase_map.shape[2] == 8 and phase_map.shape[3] == 128 and loads == 8
        if one_load_each and tiled and yield_list.shape[0] <= 8:
            return fused_body(*arguments)
        return body(*arguments)

    return chosen


def solution(mesh):
    return jax.shard_map(
        body_for(mesh),
        mesh=mesh,
        in_specs=(
            P("rve", None),
            P("rve"),
            P("rve"),
            P("rve", None),
            P("rve", "gy", "gz", None),
            P("rve", None, None, "gy", "gz", None),
            P(),
        ),
        out_specs=(P("rve", None, None, "gy", "gz", None), P("rve", None)),
        check_vma=False,
    )
```
